128 devices in a mesh: dp: 32 (over z, y, x_hi), wide: 2 (over x_lo), narrow: 2 (over core).
Axes of the slice: x: 4 (x_hi: 2, x_lo: 2; x = x_hi * 2 + x_lo), y: 4, z: 4, core: 2. Of those that a mesh axis runs over, the one named last changes fastest.
Arguments:
- hidden_in: bfloat16 [32768, 1024], P('dp', 'narrow'), may hold values from -6 to 6
- segment_ids: int32 [32768], P('dp'), may hold values from 0 to 63, never falling along the last dimension, each value on 1 to 2000 neighbouring positions
- qkv_weight: bfloat16 [1024, 16, 3, 64], P('narrow', 'wide'), may hold values from -0.1875 to 0.1875
- qv_bias: float32 [16, 2, 64], P('wide'), may hold values from -3 to 3
- out_weight: bfloat16 [16, 64, 1024], P('wide', None, 'narrow'), may hold values from -1 to 1
- out_bias: float32 [1024], P('narrow'), may hold values from -2 to 2
- norm1_gain: float32 [1024], P('narrow'), may hold values from 0.25 to 1.75
- norm1_shift: float32 [1024], P('narrow'), may hold values from -2 to 2
- up_weight: bfloat16 [1024, 4096], P('narrow', 'wide'), may hold values from -0.1875 to 0.1875
- up_bias: float32 [4096], P('wide'), may hold values from -3 to 3
- down_weight: bfloat16 [4096, 1024], P('wide', 'narrow'), may hold values from -0.1875 to 0.1875
- down_bias: float32 [1024], P('narrow'), may hold values from -2 to 2
- norm2_gain: float32 [1024], P('narrow'), may hold values from 0.25 to 1.75
- norm2_shift: float32 [1024], P('narrow'), may hold values from -2 to 2
- out_grad: bfloat16 [32768, 1024], P(('dp', 'wide'), 'narrow'), may hold values from -6 to 6
Outputs:
- hidden_out: bfloat16 [32768, 1024], P(('dp', 'wide'), 'narrow')
- input_grad: float32 [32768, 1024], P(('dp', 'wide'), 'narrow')
- qkv_weight_grad: float32 [1024, 16, 3, 64], P('narrow', 'wide')
- qv_bias_grad: float32 [16, 2, 64], P('wide')
- out_weight_grad: float32 [16, 64, 1024], P('wide', None, 'narrow')
- out_bias_grad: float32 [1024], P('narrow')
- norm1_gain_grad: float32 [1024], P('narrow')
- norm1_shift_grad: float32 [1024], P('narrow')
- up_weight_grad: float32 [1024, 4096], P('narrow', 'wide')
- up_bias_grad: float32 [4096], P('wide')
- down_weight_grad: float32 [4096, 1024], P('wide', 'narrow')
- down_bias_grad: float32 [1024], P('narrow')
- norm2_gain_grad: float32 [1024], P('narrow')
- norm2_shift_grad: float32 [1024], P('narrow')
The draws below stay inside these ranges and needn't reach their ends.
All inputs are finite; a program needn't handle non-finite values.
Results may differ from the reference program's by a relative error of at most 0.03.
Values may be sent and summed in bfloat16 or wider, within the bound.
A program may use at most 128 MiB of HBM per device.

```python
import math
import jax
import jax.numpy as jnp
import numpy as np
from jax import lax

D = 1024
H = 16
HEAD_SIZE = 64
FF = 4096
SEQ_LEN = 512
SEQ_GROUP = 2
WORD_PIECES_ALL = 32768
N_DP = 32


def levels(stream_key, dims, pieces, smallest, top_value):
    factor_of, own = 1.0, jax.random.fold_in(stream_key, 6)
    for position, shards_of in pieces:
        steps = jnp.exp(jax.random.uniform(jax.random.fold_in(own, position), (shards_of,), jnp.float32, smallest / len(pieces), top_value / len(pieces)))
        factor_of = factor_of * jnp.repeat(steps, dims[position] // shards_of).reshape([-1 if axis == position else 1 for axis in range(len(dims))])
    return factor_of


def length_profile(amount, total, reach, lean):
    portions = [(1 << 20) // math.isqrt(grade ** lean) + 1 for grade in range(2, amount + 1)]
    surplus, given = total - reach - (amount - 1), [1] * (amount - 1)
    while surplus > 0:
        candidates = [i for i in range(amount - 1) if given[i] < reach]
        mass, remaining = sum([portions[i] for i in candidates]), surplus
        for i in candidates:
            addition = min(reach - given[i], max(1, remaining * portions[i] // mass), surplus)
            given[i] = given[i] + addition
            surplus = surplus - addition
    return np.array([reach] + given)


def ragged(key, count, total, limit, lean):
    if count == 2:
        one = jax.random.randint(key, (), max(1, total - limit), min(limit, total - 1) + 1)
        return jnp.stack([one, total - one])
    tallies = jnp.asarray(length_profile(count, total, limit, lean), jnp.int32)
    twos = (count - 1) // 2
    donor, sink = tallies[1:1 + 2 * twos:2], tallies[2:2 + 2 * twos:2]
    margin = jnp.minimum(donor - 1, limit - sink)
    shifted = jax.random.randint(jax.random.fold_in(key, 1), (twos,), 0, 1 << 20) % (margin + 1)
    tallies = tallies.at[1:1 + 2 * twos:2].set(donor - shifted).at[2:2 + 2 * twos:2].set(sink + shifted)
    return tallies[jax.random.permutation(jax.random.fold_in(key, 2), count)]


def normal_values(own_key, extent, scale, most, cuts=(), dtype=jnp.bfloat16):
    values = jax.random.normal(own_key, extent, jnp.float32) * scale
    if len(cuts) > 0:
        values = levels(own_key, extent, cuts, -0.22, 0.18) * values
    return jnp.clip(values, min=-most, max=most).astype(dtype)


def setup_inputs(seed: int = 0) -> dict:
    streams_of = jax.random.split(jax.random.key(seed), 16)
    hidden_in = normal_values(streams_of[0], (WORD_PIECES_ALL, D), 1.0, 6.0, ((0, 32), (1, 2)))
    segment_ids = jnp.searchsorted(jnp.cumsum(ragged(streams_of[1], max(4, WORD_PIECES_ALL // 512), WORD_PIECES_ALL, min(2000, WORD_PIECES_ALL // 2), 1)), jnp.arange(WORD_PIECES_ALL), side="right").astype(jnp.int32)
    qkv_weight = normal_values(streams_of[2], (D, H, 3, HEAD_SIZE), D ** -0.5, 0.1875, ((0, 2), (1, 2)))
    qv_bias = normal_values(streams_of[3], (H, 2, HEAD_SIZE), 0.5, 3.0, ((0, 2),), jnp.float32)
    out_weight = normal_values(streams_of[4], (H, HEAD_SIZE, D), (D // 32) ** -0.5, 1.0, ((0, 2), (2, 2)))
    out_bias = normal_values(streams_of[5], (D,), 0.3, 2.0, ((0, 2),), jnp.float32)
    norm1_gain = jnp.clip(1.0 + 0.15 * jax.random.normal(streams_of[6], (D,), jnp.float32), 0.25, 1.75)
    norm1_shift = normal_values(streams_of[7], (D,), 0.3, 2.0, ((0, 2),), jnp.float32)
    up_weight = normal_values(streams_of[8], (D, FF), D ** -0.5, 0.1875, ((0, 2), (1, 2)))
    up_bias = normal_values(streams_of[9], (FF,), 0.5, 3.0, ((0, 2),), jnp.float32)
    down_weight = normal_values(streams_of[10], (FF, D), (FF // 4) ** -0.5, 0.1875, ((0, 2), (1, 2)))
    down_bias = normal_values(streams_of[11], (D,), 0.3, 2.0, ((0, 2),), jnp.float32)
    norm2_gain = jnp.clip(1.0 + 0.15 * jax.random.normal(streams_of[12], (D,), jnp.float32), 0.25, 1.75)
    norm2_shift = normal_values(streams_of[13], (D,), 0.3, 2.0, ((0, 2),), jnp.float32)
    out_grad = normal_values(streams_of[14], (WORD_PIECES_ALL, D), 1.0, 6.0, ((0, 64), (1, 2)))
    return {"hidden_in": hidden_in, "segment_ids": segment_ids, "qkv_weight": qkv_weight, "qv_bias": qv_bias, "out_weight": out_weight, "out_bias": out_bias, "norm1_gain": norm1_gain, "norm1_shift": norm1_shift, "up_weight": up_weight, "up_bias": up_bias, "down_weight": down_weight, "down_bias": down_bias, "norm2_gain": norm2_gain, "norm2_shift": norm2_shift, "out_grad": out_grad}


EPSILON = 1e-05
NEGATIVE = -1000000000.0
TOP_PRECISION = lax.Precision.HIGHEST

@jax.custom_vjp
def low(v):
    return lax.optimization_barrier(v.astype(jnp.bfloat16)).astype(jnp.float32)

@jax.custom_vjp
def low_back(v):
    return v

def low_keep(v):
    return (low(v), None)

def low_pass(kept, grad):
    return (grad,)

def back_keep(v):
    return (v, None)

def back_low(kept, grad):
    return (low(grad),)
low.defvjp(low_keep, low_pass)
low_back.defvjp(back_keep, back_low)

def layer_norm(values, norm_gain, norm_shift):
    center = lax.optimization_barrier(jnp.mean(values, -1, keepdims=True))
    spread = lax.optimization_barrier(jnp.mean((values - center) ** 2, -1, keepdims=True))
    return (values - center) * lax.rsqrt(spread + EPSILON) * norm_gain + norm_shift

def attend_one(blocks):
    query_rows, every_key, every_value, segment = blocks
    attention_scores = jnp.einsum('yvx,bvx->vyb', query_rows, every_key, precision=TOP_PRECISION) * HEAD_SIZE ** (-0.5)
    attention_scores = low_back(attention_scores)
    same_doc = segment[:, None] == segment[None, :]
    attention_scores = jnp.where(same_doc[None], attention_scores, NEGATIVE)
    row_peak = lax.optimization_barrier(jnp.max(attention_scores, -1, keepdims=True))
    raised = jnp.exp(attention_scores - row_peak)
    attention_weights = low(raised / lax.optimization_barrier(jnp.sum(raised, -1, keepdims=True)))
    context_rows = jnp.einsum('njv,vnz->jnz', attention_weights, every_value, precision=TOP_PRECISION)
    return low_back(low(context_rows))

def layer(learned_parameters, hidden, segment):
    qkv_weight, qv_bias, out_weight, out_bias, norm1_gain, norm1_shift, up_weight, up_bias, down_weight, down_bias, norm2_gain, norm2_shift = learned_parameters
    projected = jnp.einsum('td,dhcf->thcf', hidden, qkv_weight, precision=TOP_PRECISION)
    query_rows = low_back(low(projected[:, :, 0] + qv_bias[:, 0]))
    every_key = low_back(low(projected[:, :, 1]))
    every_value = low_back(low(projected[:, :, 2] + qv_bias[:, 1]))
    seq_count = hidden.shape[0] // SEQ_LEN
    context_rows = lax.map(jax.checkpoint(attend_one), (query_rows.reshape(seq_count, SEQ_LEN, H, HEAD_SIZE), every_key.reshape(seq_count, SEQ_LEN, H, HEAD_SIZE), every_value.reshape(seq_count, SEQ_LEN, H, HEAD_SIZE), segment.reshape(seq_count, SEQ_LEN)))
    context_rows = context_rows.reshape(hidden.shape[0], H, HEAD_SIZE)
    attention = low_back(jnp.einsum('thf,hfd->td', context_rows, out_weight, precision=TOP_PRECISION) + out_bias)
    mixed_rows = layer_norm(hidden + attention, norm1_gain, norm1_shift)
    upward = low_back(jnp.dot(low(mixed_rows), up_weight, precision=TOP_PRECISION, preferred_element_type=jnp.float32) + up_bias)
    activated = low(jax.nn.gelu(upward, approximate=False))
    downward = low_back(jnp.dot(activated, down_weight, precision=TOP_PRECISION, preferred_element_type=jnp.float32) + down_bias)
    return layer_norm(mixed_rows + downward, norm2_gain, norm2_shift)

def reference(hidden_in, segment_ids, qkv_weight, qv_bias, out_weight, out_bias, norm1_gain, norm1_shift, up_weight, up_bias, down_weight, down_bias, norm2_gain, norm2_shift, out_grad):
    learned_parameters = tuple((weight_in.astype(jnp.float32) for weight_in in (qkv_weight, qv_bias, out_weight, out_bias, norm1_gain, norm1_shift, up_weight, up_bias, down_weight, down_bias, norm2_gain, norm2_shift)))
    group_rows = SEQ_GROUP * SEQ_LEN
    inputs = hidden_in.astype(jnp.float32).reshape(N_DP, group_rows, D)
    segments = segment_ids.reshape(N_DP, group_rows)
    cotangents = out_grad.astype(jnp.float32).reshape(N_DP, group_rows, D)

    def advance(totals, blocks):
        hidden, segment, cotangent = blocks
        result, pullback = jax.vjp(lambda weights_now, hidden_now: layer(weights_now, hidden_now, segment), learned_parameters, hidden)
        weight_grads, hidden_grad = pullback(cotangent)
        totals = jax.tree.map(lambda left_side, right_side: left_side + right_side, totals, weight_grads)
        return (totals, (result, hidden_grad))
    starting = jax.tree.map(jnp.zeros_like, learned_parameters)
    totals, (results, hidden_grads) = lax.scan(advance, starting, (inputs, segments, cotangents))
    return (results.reshape(WORD_PIECES_ALL, D).astype(jnp.bfloat16), hidden_grads.reshape(WORD_PIECES_ALL, D), totals[0], totals[1], totals[2], totals[3], totals[4], totals[5], totals[6], totals[7], totals[8], totals[9], totals[10], totals[11])
```

```python
from functools import partial

import jax
import jax.numpy as jnp
from jax import lax
from jax.experimental import pallas as pl
from jax.experimental.pallas import tpu as pltpu
from jax.sharding import PartitionSpec as P

D = 1024
SEQ_LEN = 512


EPSILON = 1e-05
NEGATIVE = -1000000000.0


def for_sending(shard):
    return jax.tree.map(lambda a: a.astype(jnp.bfloat16) if a.dtype == jnp.float32 else a, shard)


def contract(left_side, right_side, left_dim, right_dim):
    return lax.dot_general(
        left_side,
        right_side,
        (((left_dim,), (right_dim,)), ((), ())),
        preferred_element_type=jnp.float32,
    )


def narrow_rows_sum(terms):
    return lax.psum_scatter(terms, "narrow", scatter_dimension=0, tiled=True)


def narrow_rows_gather(pieces):
    return lax.all_gather(for_sending(pieces), "narrow", axis=0, tiled=True).astype(pieces.dtype)


def wide_rows_gather(pieces):
    return lax.all_gather(pieces, "wide", axis=0, tiled=True)


def wide_rows_sum(left_side, right_side, right_dim, row_count):
    block = lax.slice_in_dim(left_side, 0, row_count * lax.axis_size("wide"), axis=0)
    return lax.psum_scatter(
        contract(block, right_side, 1, right_dim).astype(jnp.bfloat16),
        "wide",
        scatter_dimension=0,
        tiled=True,
    ).astype(jnp.float32)


def narrow_stats(first, second):
    return lax.psum((first, second), "narrow")


def norm_forward(rows_in, norm_gain, norm_shift):
    sums, squares = narrow_stats(jnp.sum(rows_in, -1), jnp.sum(rows_in * rows_in, -1))
    center = sums / D
    inverse = lax.rsqrt(squares / D - center * center + EPSILON)
    normed = (rows_in - center[:, None]) * inverse[:, None]
    return (normed * norm_gain + norm_shift, normed, inverse)


def norm_backward(grad_rows, normed, inverse, norm_gain):
    scaled = grad_rows * norm_gain
    first, second = narrow_stats(jnp.sum(scaled, -1), jnp.sum(scaled * normed, -1))
    return inverse[:, None] * (scaled - first[:, None] / D - normed * (second[:, None] / D))


def gain_parts(grad_rows, normed):
    return (jnp.sum(grad_rows * normed, 0), jnp.sum(grad_rows, 0))


def by_sequence(tensor, seq_len):
    return tensor.reshape((tensor.shape[0] // seq_len, seq_len) + tensor.shape[1:])


def masked_scores(tile_probe_vectors, block_keys, segment_block, score_scale):
    attention_scores = (
        jnp.einsum(
            "yvx,bvx->vyb", tile_probe_vectors, block_keys, preferred_element_type=jnp.float32
        )
        * score_scale
    )
    same_doc = segment_block[:, None] == segment_block[None, :]
    return jnp.where(same_doc[None], attention_scores, NEGATIVE)


def attend(query_rows, every_key, every_value, segment, seq_len, score_scale):
    row_count, head_count, head_width = query_rows.shape

    def one_sequence(blocks):
        tile_probe_vectors, block_keys, block_values, segment_block = blocks
        attention_scores = masked_scores(tile_probe_vectors, block_keys, segment_block, score_scale)
        row_peak = jnp.max(attention_scores, -1, keepdims=True)
        raised = jnp.exp(attention_scores - row_peak)
        row_total = jnp.sum(raised, -1, keepdims=True)
        attention_weights = (raised / row_total).astype(jnp.bfloat16)
        context_rows = jnp.einsum(
            "njv,vnz->jnz", attention_weights, block_values, preferred_element_type=jnp.float32
        )
        return (context_rows.astype(jnp.bfloat16), (row_peak + jnp.log(row_total))[..., 0])

    context_rows, logarithm_normalizer = lax.map(
        one_sequence,
        (
            by_sequence(query_rows, seq_len),
            by_sequence(every_key, seq_len),
            by_sequence(every_value, seq_len),
            by_sequence(segment, seq_len),
        ),
    )
    return (context_rows.reshape(row_count, head_count * head_width), logarithm_normalizer)


def attend_back(
    query_rows,
    every_key,
    every_value,
    segment,
    logarithm_normalizer,
    grad_context,
    seq_len,
    score_scale,
):
    row_count, head_count, head_width = query_rows.shape

    def one_sequence(blocks):
        tile_probe_vectors, block_keys, block_values, segment_block, total_block, gradient_block = (
            blocks
        )
        attention_scores = masked_scores(tile_probe_vectors, block_keys, segment_block, score_scale)
        probs = jnp.exp(attention_scores - total_block[..., None])
        grad_values = jnp.einsum(
            "dvz,vdq->zdq",
            probs.astype(jnp.bfloat16),
            gradient_block,
            preferred_element_type=jnp.float32,
        )
        grad_probs = jnp.einsum(
            "yvx,bvx->vyb", gradient_block, block_values, preferred_element_type=jnp.float32
        )
        inner = jnp.sum(grad_probs * probs, -1, keepdims=True)
        logit_sensitivity = (probs * (grad_probs - inner)).astype(jnp.bfloat16)
        grad_queries = (
            jnp.einsum(
                "njv,vnz->jnz", logit_sensitivity, block_keys, preferred_element_type=jnp.float32
            )
            * score_scale
        )
        grad_keys = (
            jnp.einsum(
                "dvz,vdq->zdq",
                logit_sensitivity,
                tile_probe_vectors,
                preferred_element_type=jnp.float32,
            )
            * score_scale
        )
        return jnp.stack(
            [
                grad_queries.astype(jnp.bfloat16),
                grad_keys.astype(jnp.bfloat16),
                grad_values.astype(jnp.bfloat16),
            ],
            2,
        )

    stacked = lax.map(
        one_sequence,
        (
            by_sequence(query_rows, seq_len),
            by_sequence(every_key, seq_len),
            by_sequence(every_value, seq_len),
            by_sequence(segment, seq_len),
            logarithm_normalizer,
            by_sequence(grad_context, seq_len),
        ),
    )
    return stacked.reshape(row_count, head_count * 3 * head_width)


def split_qkv(projected, qv_bias, row_count, heads_here, head_width):
    qkv_four = projected.reshape(row_count, heads_here, 3, head_width)
    query_rows = (qkv_four[:, :, 0] + qv_bias[:, 0]).astype(jnp.bfloat16)
    every_key = qkv_four[:, :, 1].astype(jnp.bfloat16)
    every_value = (qkv_four[:, :, 2] + qv_bias[:, 1]).astype(jnp.bfloat16)
    return (query_rows, every_key, every_value)


def bias_pair(grad_qkv, heads_here, head_width):
    qkv_sums = jnp.sum(grad_qkv, 0, dtype=jnp.float32).reshape(heads_here, 3, head_width)
    return jnp.stack([qkv_sums[:, 0], qkv_sums[:, 2]], 1)


MESH = pl.DeviceIdType.MESH
BF = jnp.bfloat16
F32 = jnp.float32
PACK = 512


def partner_table():
    dp = lax.axis_index("dp")
    z, y, xh = dp // 8, (dp // 2) % 4, dp % 2
    wide, narrow = lax.axis_index("wide"), lax.axis_index("narrow")

    def at(z, y, xh):
        return (z * 8 + y * 2 + xh, wide, narrow)

    def parity(v):
        return (v % 2 + v // 2) % 2

    return {
        "y1": (at(z, y + 1 - 2 * (y % 2), xh), parity(y)),
        "z1": (at(z + 1 - 2 * (z % 2), y, xh), parity(z)),
        "y3": (at(z, 3 - y, xh), y // 2),
        "z3": (at(3 - z, y, xh), z // 2),
        "xh": (at(z, y, 1 - xh), xh),
        "wide": ((dp, 1 - wide, narrow), wide),
    }


ORDERS = (
    ("y1", "z1", "y3", "z3"),
    ("z1", "y3", "z3", "y1"),
    ("y3", "z3", "y1", "z1"),
    ("z3", "y1", "z1", "y3"),
)
SMALL_ORDER = ("wide", "y1", "z1", "y3", "z3", "xh")


class Summing:
    def __init__(self, buf, recv, out, send_sem, recv_sem, base, rows, recv_base, table):
        self.buf, self.recv, self.out = buf, recv, out
        self.send_sem, self.recv_sem, self.table = send_sem, recv_sem, table
        self.quarter = rows // 4
        self.offsets, self.places = [], []
        place = recv_base
        for q, order in enumerate(ORDERS):
            offset, size = base + q * self.quarter, self.quarter
            trail, slots = [offset], []
            for name in order:
                size = size // 2
                offset = pl.multiple_of(offset + table[name][1] * size, 16)
                trail.append(offset)
                slots.append(place)
                place += size
            slots.append(place)
            place += size
            self.offsets.append(trail)
            self.places.append(slots)
        self.sent = []

    def size(self, level):
        return self.quarter >> level

    def copy(self, q, step, src, dst, name):
        return pltpu.make_async_remote_copy(
            src_ref=src,
            dst_ref=dst,
            send_sem=self.send_sem.at[q, step],
            recv_sem=self.recv_sem.at[q, step],
            device_id=self.table[name][0],
            device_id_type=MESH,
        )

    def make(self, q, step):
        if step < 4:
            name, size = ORDERS[q][step], self.size(step + 1)
            start = self.offsets[q][step] + (1 - self.table[name][1]) * size
            src = self.buf.at[pl.ds(pl.multiple_of(start, 16), size), :]
            dst = self.recv.at[pl.ds(self.places[q][step], size), :]
        elif step == 4:
            name, size = "xh", self.size(4)
            src = self.buf.at[pl.ds(self.offsets[q][4], size), :]
            dst = self.recv.at[pl.ds(self.places[q][4], size), :]
        else:
            level = 9 - step
            name, size = ORDERS[q][level - 1], self.size(level)
            src = self.out.at[pl.ds(self.offsets[q][level], size), :]
            dst = src
        return self.copy(q, step, src, dst, name)

    def begin(self, q, step):
        copy = self.make(q, step)
        copy.start()
        self.sent.append(copy)

    def take(self, q, step):
        self.make(q, step).wait_recv()
        if step <= 4:
            level = min(step + 1, 4)
            size = self.size(level)
            target = self.out if step == 4 else self.buf
            chunk = 32
            offset, place = self.offsets[q][level], self.places[q][step]

            def add(i, carry):
                here = pl.ds(pl.multiple_of(offset + i * chunk, 16), chunk)
                there = pl.ds(pl.multiple_of(place + i * chunk, 16), chunk)
                total = self.buf[here, :].astype(F32) + self.recv[there, :].astype(F32)
                target[here, :] = total.astype(BF)
                return carry

            lax.fori_loop(0, size // chunk, add, 0)

    def open(self):
        for q in range(4):
            self.begin(q, 0)

    def advance(self, step):
        for q in range(4):
            self.take(q, step)
            if step < 8:
                self.begin(q, step + 1)

    def close(self):
        for copy in self.sent:
            copy.wait_send()


def sum_kernel(buf_in, small_in, out, small_out, buf, recv, small_recv, ss, rs, small_ss, small_rs):
    table = partner_table()
    barrier = pltpu.get_barrier_semaphore()
    for device, _ in table.values():
        pl.semaphore_signal(barrier, inc=1, device_id=device, device_id_type=MESH)
    pl.semaphore_wait(barrier, len(table))
    rows = buf_in.shape[0]
    work = Summing(buf_in, recv, out, ss, rs, 0, rows, 0, table)
    work.buf = buf
    chunk = 64

    def stage(i, carry):
        here = pl.ds(pl.multiple_of(i * chunk, 16), chunk)
        buf[here, :] = buf_in[here, :]
        return carry

    lax.fori_loop(0, rows // chunk, stage, 0)
    work.open()
    small_sent = []
    held = small_in[...]
    for step in range(9):
        if step < len(SMALL_ORDER):
            small_out[step] = held
            first = 8 if step == 0 else 0
            copy = pltpu.make_async_remote_copy(
                src_ref=small_out.at[step, pl.ds(first, 16 - first)],
                dst_ref=small_recv.at[step, pl.ds(first, 16 - first)],
                send_sem=small_ss.at[step],
                recv_sem=small_rs.at[step],
                device_id=table[SMALL_ORDER[step]][0],
                device_id_type=MESH,
            )
            copy.start()
            small_sent.append(copy)
        work.advance(step)
        if step < len(SMALL_ORDER):
            copy.wait_recv()
            if step == 0:
                top = held[:8]
                held = jnp.concatenate([top, held[8:] + small_recv[0, 8:, :]], 0)
            else:
                held = held + small_recv[step]
    small_out[len(SMALL_ORDER)] = held
    work.close()
    for copy in small_sent:
        copy.wait_send()


def sum_over_dp(packed, small):
    rows = packed.shape[0]
    steps = len(SMALL_ORDER)
    vmem = pl.BlockSpec(memory_space=pltpu.VMEM)
    out, small_out = pl.pallas_call(
        sum_kernel,
        out_shape=(
            jax.ShapeDtypeStruct((rows, PACK), BF),
            jax.ShapeDtypeStruct((steps + 1, 16, PACK), F32),
        ),
        in_specs=[vmem, vmem],
        out_specs=(vmem, vmem),
        scratch_shapes=[
            pltpu.VMEM((rows, PACK), BF),
            pltpu.VMEM((rows, PACK), BF),
            pltpu.VMEM((steps, 16, PACK), F32),
            pltpu.SemaphoreType.DMA((4, 9)),
            pltpu.SemaphoreType.DMA((4, 9)),
            pltpu.SemaphoreType.DMA((steps,)),
            pltpu.SemaphoreType.DMA((steps,)),
        ],
        compiler_params=pltpu.CompilerParams(
            collective_id=1, has_side_effects=True, vmem_limit_bytes=56 * 2**20
        ),
    )(packed, small)
    return out, small_out[steps]


def pack_columns(matrix):
    return [matrix[:, i : i + PACK] for i in range(0, matrix.shape[1], PACK)]


def per_device(
    hidden_in,
    segment_ids,
    qkv_weight,
    qv_bias,
    out_weight,
    out_bias,
    norm1_gain,
    norm1_shift,
    up_weight,
    up_bias,
    down_weight,
    down_bias,
    norm2_gain,
    norm2_shift,
    out_grad,
):
    token_count, half_width = hidden_in.shape
    heads_here = qkv_weight.shape[1]
    head_width = qkv_weight.shape[3]
    wide_rows = out_grad.shape[0]
    narrow_count = lax.axis_size("narrow")
    narrow_at = lax.axis_index("narrow")
    wide_start = lax.axis_index("wide") * wide_rows
    score_scale = head_width ** (-0.5)
    qkv_flat = qkv_weight.reshape(half_width, heads_here * 3 * head_width)
    out_flat = out_weight.reshape(heads_here * head_width, half_width)
    gelu_exact = partial(jax.nn.gelu, approximate=False)
    att_rows = token_count // narrow_count
    qkv_part = narrow_rows_sum(jnp.dot(hidden_in, qkv_flat, preferred_element_type=jnp.float32))
    att_segment = lax.dynamic_slice_in_dim(segment_ids, narrow_at * att_rows, att_rows)
    query_rows, every_key, every_value = split_qkv(
        qkv_part, qv_bias, att_rows, heads_here, head_width
    )
    context_rows, logarithm_normalizer = attend(
        query_rows, every_key, every_value, att_segment, SEQ_LEN, score_scale
    )
    context_full = narrow_rows_gather(context_rows)
    hidden_mine = lax.dynamic_slice_in_dim(hidden_in, wide_start, wide_rows, 0).astype(jnp.float32)
    attn_mine = wide_rows_sum(context_full, out_flat, 0, wide_rows) + out_bias
    norm1_mine, normed1, inverse1 = norm_forward(hidden_mine + attn_mine, norm1_gain, norm1_shift)
    mixed_full = wide_rows_gather(norm1_mine.astype(jnp.bfloat16))
    upward = (
        narrow_rows_sum(jnp.dot(mixed_full, up_weight, preferred_element_type=jnp.float32))
        + up_bias
    )
    activated_full = narrow_rows_gather(gelu_exact(upward).astype(jnp.bfloat16))
    downward = wide_rows_sum(activated_full, down_weight, 0, wide_rows) + down_bias
    out_rows, normed2, inverse2 = norm_forward(norm1_mine + downward, norm2_gain, norm2_shift)
    hidden_out = out_rows.astype(jnp.bfloat16)
    cotangent = out_grad.astype(jnp.float32)
    grad_res2 = norm_backward(cotangent, normed2, inverse2, norm2_gain)
    gain2_part, shift2_part = gain_parts(cotangent, normed2)
    grad_down_full = wide_rows_gather(grad_res2.astype(jnp.bfloat16))
    grad_hidden = narrow_rows_sum(contract(grad_down_full, down_weight, 1, 1))
    gelu_value, gelu_pull = jax.vjp(gelu_exact, upward)
    expansion_cotangent_entire = narrow_rows_gather(gelu_pull(grad_hidden)[0].astype(jnp.bfloat16))
    down_weight_grad = contract(activated_full, grad_down_full, 0, 0)
    down_bias_grad = jnp.sum(grad_down_full, 0, dtype=jnp.float32)
    up_weight_grad = contract(mixed_full, expansion_cotangent_entire, 0, 0)
    up_bias_grad = jnp.sum(expansion_cotangent_entire, 0, dtype=jnp.float32)
    grad_mixed = grad_res2 + wide_rows_sum(expansion_cotangent_entire, up_weight, 1, wide_rows)
    grad_res1 = norm_backward(grad_mixed, normed1, inverse1, norm1_gain)
    gain1_part, shift1_part = gain_parts(grad_mixed, normed1)
    grad_attn_full = wide_rows_gather(grad_res1.astype(jnp.bfloat16))
    out_weight_grad = contract(context_full, grad_attn_full, 0, 0).reshape(
        heads_here, head_width, half_width
    )
    out_bias_grad = jnp.sum(grad_attn_full, 0, dtype=jnp.float32)
    grad_context = narrow_rows_sum(contract(grad_attn_full, out_flat, 1, 1))
    grad_context = grad_context.astype(jnp.bfloat16).reshape(att_rows, heads_here, head_width)
    grad_qkv = attend_back(
        query_rows,
        every_key,
        every_value,
        att_segment,
        logarithm_normalizer,
        grad_context,
        SEQ_LEN,
        score_scale,
    )
    grad_qkv_full = narrow_rows_gather(grad_qkv)
    qkv_weight_grad = contract(hidden_in, grad_qkv_full, 0, 0).reshape(
        half_width, heads_here, 3, head_width
    )
    qv_bias_grad = bias_pair(grad_qkv_full, heads_here, head_width)
    input_grad = grad_res1 + wide_rows_sum(grad_qkv_full, qkv_flat, 1, wide_rows)
    packed = jnp.concatenate(
        [
            piece.astype(BF)
            for piece in pack_columns(qkv_weight_grad.reshape(half_width, -1))
            + [out_weight_grad.reshape(-1, half_width)]
            + pack_columns(up_weight_grad)
            + [down_weight_grad]
        ],
        0,
    )
    small = jnp.concatenate(
        [
            qv_bias_grad.reshape(-1, PACK),
            out_bias_grad[None],
            down_bias_grad[None],
            up_bias_grad.reshape(-1, PACK),
            jnp.stack([gain1_part, shift1_part, gain2_part, shift2_part]),
            jnp.zeros((4, PACK), F32),
        ],
        0,
    )
    total, small = sum_over_dp(packed, small)
    total = total.astype(F32)
    heads_rows = heads_here * head_width
    qkv_rows = 3 * heads_rows
    up_start = qkv_rows + heads_rows
    up_rows = up_weight.shape[1] // PACK * half_width
    blocks = lambda rows: jnp.concatenate(jnp.split(rows, rows.shape[0] // half_width, 0), 1)
    qv_bias_sum = small[0:2].reshape(heads_here, 2, head_width)
    summed = (
        blocks(total[:qkv_rows]).reshape(half_width, heads_here, 3, head_width),
        qv_bias_sum,
        total[qkv_rows:up_start].reshape(heads_here, head_width, half_width),
        small[2],
        blocks(total[up_start : up_start + up_rows]),
        small[4:8].reshape(-1),
        total[up_start + up_rows :],
        small[3],
    )
    norm_sums = (small[8], small[9], small[10], small[11])
    return (
        hidden_out,
        input_grad,
        summed[0],
        summed[1],
        summed[2],
        summed[3],
        norm_sums[0],
        norm_sums[1],
        summed[4],
        summed[5],
        summed[6],
        summed[7],
        norm_sums[2],
        norm_sums[3],
    )


def solution(mesh):
    return jax.shard_map(
        per_device,
        mesh=mesh,
        in_specs=(
            P("dp", "narrow"),
            P("dp"),
            P("narrow", "wide", None, None),
            P("wide", None, None),
            P("wide", None, "narrow"),
            P("narrow"),
            P("narrow"),
            P("narrow"),
            P("narrow", "wide"),
            P("wide"),
            P("wide", "narrow"),
            P("narrow"),
            P("narrow"),
            P("narrow"),
            P(("dp", "wide"), "narrow"),
        ),
        out_specs=(
            P(("dp", "wide"), "narrow"),
            P(("dp", "wide"), "narrow"),
            P("narrow", "wide", None, None),
            P("wide", None, None),
            P("wide", None, "narrow"),
            P("narrow"),
            P("narrow"),
            P("narrow"),
            P("narrow", "wide"),
            P("wide"),
            P("wide", "narrow"),
            P("narrow"),
            P("narrow"),
            P("narrow"),
        ),
        check_vma=False,
    )
```

```python
import jax
import jax.numpy as jnp
from jax import lax
from jax.experimental import pallas as pl
from jax.experimental.pallas import tpu as pltpu
from jax.sharding import PartitionSpec as P

EPSILON = 1e-05
NEGATIVE = -1000000000.0
MESH = pl.DeviceIdType.MESH
BF = jnp.bfloat16
F32 = jnp.float32
PACK = 512


def partner_table():
    dp = lax.axis_index("dp")
    z, y, xh = dp // 8, (dp // 2) % 4, dp % 2
    wide, narrow = lax.axis_index("wide"), lax.axis_index("narrow")

    def at(z, y, xh):
        return (z * 8 + y * 2 + xh, wide, narrow)

    def parity(v):
        return (v % 2 + v // 2) % 2

    return {
        "y1": (at(z, y + 1 - 2 * (y % 2), xh), parity(y)),
        "z1": (at(z + 1 - 2 * (z % 2), y, xh), parity(z)),
        "y3": (at(z, 3 - y, xh), y // 2),
        "z3": (at(3 - z, y, xh), z // 2),
        "xh": (at(z, y, 1 - xh), xh),
        "wide": ((dp, 1 - wide, narrow), wide),
    }


ORDERS = (
    ("y1", "z1", "y3", "z3"),
    ("z1", "y3", "z3", "y1"),
    ("y3", "z3", "y1", "z1"),
    ("z3", "y1", "z1", "y3"),
)
SMALL_ORDER = ("wide", "y1", "z1", "y3", "z3", "xh")


class Summing:
    def __init__(self, buf, recv, out, send_sem, recv_sem, base, rows, recv_base, table):
        self.buf, self.recv, self.out = buf, recv, out
        self.send_sem, self.recv_sem, self.table = send_sem, recv_sem, table
        self.quarter = rows // 4
        self.offsets, self.places = [], []
        place = recv_base
        for q, order in enumerate(ORDERS):
            offset, size = base + q * self.quarter, self.quarter
            trail, slots = [offset], []
            for name in order:
                size = size // 2
                offset = pl.multiple_of(offset + table[name][1] * size, 16)
                trail.append(offset)
                slots.append(place)
                place += size
            slots.append(place)
            place += size
            self.offsets.append(trail)
            self.places.append(slots)
        self.sent = []

    def size(self, level):
        return self.quarter >> level

    def copy(self, q, step, src, dst, name):
        return pltpu.make_async_remote_copy(
            src_ref=src,
            dst_ref=dst,
            send_sem=self.send_sem.at[q, step],
            recv_sem=self.recv_sem.at[q, step],
            device_id=self.table[name][0],
            device_id_type=MESH,
        )

    def make(self, q, step):
        if step < 4:
            name, size = ORDERS[q][step], self.size(step + 1)
            start = self.offsets[q][step] + (1 - self.table[name][1]) * size
            src = self.buf.at[pl.ds(pl.multiple_of(start, 16), size), :]
            dst = self.recv.at[pl.ds(self.places[q][step], size), :]
        elif step == 4:
            name, size = "xh", self.size(4)
            src = self.buf.at[pl.ds(self.offsets[q][4], size), :]
            dst = self.recv.at[pl.ds(self.places[q][4], size), :]
        else:
            level = 9 - step
            name, size = ORDERS[q][level - 1], self.size(level)
            src = self.out.at[pl.ds(self.offsets[q][level], size), :]
            dst = src
        return self.copy(q, step, src, dst, name)

    def begin(self, q, step):
        copy = self.make(q, step)
        copy.start()
        self.sent.append(copy)

    def take(self, q, step):
        self.make(q, step).wait_recv()
        if step <= 4:
            level = min(step + 1, 4)
            size = self.size(level)
            target = self.out if step == 4 else self.buf
            chunk = 32
            offset, place = self.offsets[q][level], self.places[q][step]

            def add(i, carry):
                here = pl.ds(pl.multiple_of(offset + i * chunk, 16), chunk)
                there = pl.ds(pl.multiple_of(place + i * chunk, 16), chunk)
                total = self.buf[here, :].astype(F32) + self.recv[there, :].astype(F32)
                target[here, :] = total.astype(BF)
                return carry

            lax.fori_loop(0, size // chunk, add, 0)

    def open(self):
        for q in range(4):
            self.begin(q, 0)

    def advance(self, step):
        for q in range(4):
            self.take(q, step)
            if step < 8:
                self.begin(q, step + 1)

    def close(self):
        for copy in self.sent:
            copy.wait_send()


def sum_kernel(buf_in, small_in, out, small_out, buf, recv, small_recv, ss, rs, small_ss, small_rs):
    table = partner_table()
    barrier = pltpu.get_barrier_semaphore()
    for device, _ in table.values():
        pl.semaphore_signal(barrier, inc=1, device_id=device, device_id_type=MESH)
    pl.semaphore_wait(barrier, len(table))
    rows = buf_in.shape[0]
    work = Summing(buf_in, recv, out, ss, rs, 0, rows, 0, table)
    work.buf = buf
    chunk = 64

    def stage(i, carry):
        here = pl.ds(pl.multiple_of(i * chunk, 16), chunk)
        buf[here, :] = buf_in[here, :]
        return carry

    lax.fori_loop(0, rows // chunk, stage, 0)
    work.open()
    small_sent = []
    held = small_in[...]
    for step in range(9):
        if step < len(SMALL_ORDER):
            small_out[step] = held
            first = 24 if step == 0 else 0
            copy = pltpu.make_async_remote_copy(
                src_ref=small_out.at[step, pl.ds(first, 32 - first)],
                dst_ref=small_recv.at[step, pl.ds(first, 32 - first)],
                send_sem=small_ss.at[step],
                recv_sem=small_rs.at[step],
                device_id=table[SMALL_ORDER[step]][0],
                device_id_type=MESH,
            )
            copy.start()
            small_sent.append(copy)
        work.advance(step)
        if step < len(SMALL_ORDER):
            copy.wait_recv()
            if step == 0:
                top = held[:24]
                held = jnp.concatenate([top, held[24:] + small_recv[0, 24:, :]], 0)
            else:
                held = held + small_recv[step]
    small_out[len(SMALL_ORDER)] = held
    work.close()
    for copy in small_sent:
        copy.wait_send()


def sum_over_dp(packed, small):
    rows = packed.shape[0]
    steps = len(SMALL_ORDER)
    vmem = pl.BlockSpec(memory_space=pltpu.VMEM)
    out, small_out = pl.pallas_call(
        sum_kernel,
        out_shape=(
            jax.ShapeDtypeStruct((rows, PACK), BF),
            jax.ShapeDtypeStruct((steps + 1, 32, 256), F32),
        ),
        in_specs=[vmem, vmem],
        out_specs=(vmem, vmem),
        scratch_shapes=[
            pltpu.VMEM((rows, PACK), BF),
            pltpu.VMEM((rows, PACK), BF),
            pltpu.VMEM((steps, 32, 256), F32),
            pltpu.SemaphoreType.DMA((4, 9)),
            pltpu.SemaphoreType.DMA((4, 9)),
            pltpu.SemaphoreType.DMA((steps,)),
            pltpu.SemaphoreType.DMA((steps,)),
        ],
        compiler_params=pltpu.CompilerParams(
            collective_id=1, has_side_effects=True, vmem_limit_bytes=56 * 2**20
        ),
    )(packed, small)
    return out, small_out[steps]


SEQ = 512
PART = 256
ROWS_SMALL = 32
SMALL_QKV, SMALL_UP, SMALL_OUT, SMALL_DOWN, SMALL_NORM = 0, 6, 14, 16, 24
HALF_ROOT = 0.7071067811865476
INV_ROOT_2PI = 0.3989422804014327
QKV_ROWS, OUT_ROWS, UP_ROWS, DOWN_ROWS = 1536, 512, 2048, 2048
PACKED_ROWS = QKV_ROWS + OUT_ROWS + UP_ROWS + DOWN_ROWS
UP_BASE, DOWN_BASE, QKV_BASE, OUT_BASE = 0, 2048, 4096, 5632


def mm(a, b):
    return lax.dot_general(a, b, (((1,), (0,)), ((), ())), preferred_element_type=F32)


def mm_right(a, b):
    return lax.dot_general(a, b, (((1,), (1,)), ((), ())), preferred_element_type=F32)


def mm_left(a, b):
    return lax.dot_general(a, b, (((0,), (0,)), ((), ())), preferred_element_type=F32)


def span(start, size, step=128):
    return pl.ds(pl.multiple_of(start, step), size)


def tiles(count, body):
    lax.fori_loop(0, count, lambda i, carry: (body(i), carry)[1], 0)


class Net:
    def __init__(self, send_sem, recv_sem):
        self.send_sem, self.recv_sem, self.sent = send_sem, recv_sem, []

    def send(self, src, dst, device):
        i = len(self.sent)
        copy = pltpu.make_async_remote_copy(
            src_ref=src,
            dst_ref=dst,
            send_sem=self.send_sem.at[i],
            recv_sem=self.recv_sem.at[i],
            device_id=device,
            device_id_type=MESH,
        )
        copy.start()
        self.sent.append(copy)
        return copy

    def close(self):
        for copy in self.sent:
            copy.wait_send()


MESSAGES = 64


def layer_kernel(
    hid, seg_row, seg_col, qkv_w, qv_b, out_w, out_b, gain1, shift1, up_w, up_b, dn_w, dn_b,
    gain2, shift2, dy,
    hid_out, in_grad, packed, small,
    hid_o, qkvw_o, outw_o, upw_o, dnw_o,
    qs, ks, vs, probs, ctx_own, ctx_o,
    rs_send, rs_recv, stat_send, stat_recv,
    acc, res1, res2, inv1, pre,
    mixed_own, mixed_o, act_own, act_o, slope, gd_own, gd_o, gu_own, gu_o, ga_own, ga_o,
    dctx, dqkv_own, dqkv_o,
    send_sem, recv_sem,
):
    dp, w, n = lax.axis_index("dp"), lax.axis_index("wide"), lax.axis_index("narrow")
    twin, peer = (dp, w, 1 - n), (dp, 1 - w, n)
    barrier = pltpu.get_barrier_semaphore()
    for device in (twin, peer):
        pl.semaphore_signal(barrier, inc=1, device_id=device, device_id_type=MESH)
    pl.semaphore_wait(barrier, 2)
    net = Net(send_sem, recv_sem)
    seq_of = (w, 1 - w)
    base_of = (w * SEQ, (1 - w) * SEQ)
    lane = lax.broadcasted_iota(jnp.int32, (1, 128), 1)
    low = lane < 64
    picks = (low.astype(F32).astype(BF), (lane >= 64).astype(F32).astype(BF))
    scale = 0.125
    width = hid.shape[1]
    features = 2.0 * width

    hid_got = [None, None]
    hid_got[1] = net.send(hid.at[span(base_of[1], SEQ)], hid_o.at[1], twin)
    qkvw_got = net.send(qkv_w.at[:, span((1 - n) * 768, 768)], qkvw_o, twin)
    hid_got[0] = net.send(hid.at[span(base_of[0], SEQ)], hid_o.at[0], twin)
    upw_got = net.send(up_w.at[:, span((1 - n) * 1024, 1024)], upw_o, twin)
    dnw_got = net.send(dn_w.at[span((1 - n) * 1024, 1024), :], dnw_o, twin)
    outw_got = net.send(out_w.at[span((1 - n) * 256, 256), :], outw_o, twin)

    small[...] = jnp.zeros_like(small)

    def project(s):
        def block(i):
            p, r = i // 2, i % 2
            here = span(r * PART, PART)
            got = mm(hid[span(base_of[s] + r * PART, PART), :], qkv_w[:, span(n * 768 + p * 384, 384)])
            got += mm(hid_o[s, here, :], qkvw_o[:, span(p * 384, 384)])
            b0, b1, b2 = got[:, :128], got[:, 128:256], got[:, 256:]
            first, second = qv_b[pl.ds(n * 4 + 2 * p, 1), :], qv_b[pl.ds(n * 4 + 2 * p + 1, 1), :]
            q_bias = jnp.where(low, first, pltpu.roll(second, 64, 1))
            v_bias = jnp.where(low, pltpu.roll(first, 64, 1), second)
            qs[s, p, here, :] = (jnp.where(low, b0, b1) + q_bias).astype(BF)
            ks[s, p, here, :] = jnp.where(low, pltpu.roll(b0, 64, 1), pltpu.roll(b2, 64, 1)).astype(BF)
            vs[s, p, here, :] = (jnp.where(low, b1, b2) + v_bias).astype(BF)

        tiles(4, block)

    def attend_forward(s):
        def block(i):
            p, r = i // 2, i % 2
            here = span(r * PART, PART)
            q, k, v = qs[s, p, here, :], ks[s, p], vs[s, p]
            same = seg_col[span(base_of[s] + r * PART, PART), :] == seg_row[pl.ds(seq_of[s], 1), :]
            parts = []
            for h in range(2):
                score = jnp.where(same, mm_right(q * picks[h], k) * scale, NEGATIVE)
                raised = jnp.exp(score - jnp.max(score, -1, keepdims=True))
                weight = (raised / jnp.sum(raised, -1, keepdims=True)).astype(BF)
                probs[s, p * 2 + h, here, :] = weight
                parts.append(mm(weight, v))
            ctx_own[s, here, span(p * 128, 128)] = jnp.where(low, parts[0], parts[1]).astype(BF)

        tiles(4, block)
        return net.send(ctx_own.at[s], ctx_o.at[s], twin)

    def out_rows(s, c):
        here = pl.ds(c * PART, PART)
        return mm(ctx_own[s, here, :], out_w[span(n * 256, 256), :]) + mm(
            ctx_o[s, here, :], out_w[span((1 - n) * 256, 256), :]
        )

    def reduce_send(k, c, rows):
        here = pl.ds(c * PART, PART)
        rs_send[k, here, :] = rows.astype(BF)
        return net.send(rs_send.at[k, here], rs_recv.at[k, here], peer)

    def stat_pack(values):
        values = list(values) + [values[-1]] * (4 - len(values))
        return jnp.where(
            lane < 64,
            jnp.where(lane < 32, values[0], values[1]),
            jnp.where(lane < 96, values[2], values[3]),
        )

    def stat_exchange(k, c):
        here = pl.ds(c * PART, PART)
        return net.send(stat_send.at[k, here], stat_recv.at[k, here], twin)

    def stat_total(k, rows, i):
        return stat_send[k, rows, 32 * i : 32 * i + 1] + stat_recv[k, rows, 32 * i : 32 * i + 1]

    def row_sum(values):
        return jnp.sum(values, -1, keepdims=True)

    def column_add(row, values):
        for j in range(2):
            small[row + j : row + j + 1, :] += jnp.sum(
                values[:, j * 256 : (j + 1) * 256], 0, keepdims=True
            )

    STEP = 64

    def spread(own, c):
        here = pl.ds(c * PART, PART)
        across = net.send(own[0].at[0, here], own[0].at[1, here], peer)
        beside = net.send(own[0].at[0, here], own[1].at[0, here], twin)
        return across, beside

    def pass_on(own, c, across):
        here = pl.ds(c * PART, PART)
        across.wait_recv()
        return net.send(own[0].at[1, here], own[1].at[1, here], twin)

    hid_got[1].wait_recv()
    qkvw_got.wait_recv()
    project(1)
    ctx_got1 = attend_forward(1)
    hid_got[0].wait_recv()
    project(0)
    ctx_got1.wait_recv()
    rs1 = [reduce_send(0, c, out_rows(1, c)) for c in range(2)]
    ctx_got0 = attend_forward(0)
    ctx_got0.wait_recv()
    for c in range(2):
        acc[pl.ds(c * PART, PART), :] = out_rows(0, c)

    stats1 = []
    for c in range(2):
        rs1[c].wait_recv()

        def gather(i):
            rows = span(c * PART + i * STEP, STEP, 64)
            r = hid[span(base_of[0] + c * PART + i * STEP, STEP, 64), :].astype(F32)
            r = r + acc[rows, :] + rs_recv[0, rows, :].astype(F32) + out_b[...]
            res1[rows, :] = r
            stat_send[0, rows, :] = stat_pack([row_sum(r), row_sum(r * r)])

        tiles(PART // STEP, gather)
        stats1.append(stat_exchange(0, c))
    mixed = (mixed_own, mixed_o)
    mixed_sent = []
    for c in range(2):
        stats1[c].wait_recv()

        def normalize(i):
            rows = span(c * PART + i * STEP, STEP, 64)
            center = stat_total(0, rows, 0) / features
            inverse = lax.rsqrt(stat_total(0, rows, 1) / features - center * center + EPSILON)
            normed = (res1[rows, :] - center) * inverse
            res1[rows, :] = normed
            inv1[rows, :] = jnp.broadcast_to(inverse, (STEP, 128))
            mixed_own[0, rows, :] = (normed * gain1[...] + shift1[...]).astype(BF)

        tiles(PART // STEP, normalize)
        mixed_sent.append(spread(mixed, c))

    upw_got.wait_recv()

    def expand(s, c):
        here = pl.ds(c * PART, PART)
        pre[...] = mm(mixed_own[s, here, :], up_w[:, span(n * 1024, 1024)]) + mm(
            mixed_o[s, here, :], upw_o[...]
        )

        def bend(i):
            rows = span(i * 32, 32, 32)
            there = span(c * PART + i * 32, 32, 32)
            u = pre[rows, :] + up_b[:, span(n * 1024, 1024)]
            share = 0.5 * (1.0 + lax.erf(u * HALF_ROOT))
            act_own[s, there, :] = (u * share).astype(BF)
            slope[s, there, :] = (share + u * (INV_ROOT_2PI * jnp.exp(-0.5 * u * u))).astype(BF)

        tiles(PART // 32, bend)
        return net.send(act_own.at[s, here], act_o.at[s, here], twin)

    act_got = {}
    for c in range(2):
        mixed_sent[c][1].wait_recv()
        act_got[0, c] = expand(0, c)
    for c in range(2):
        pass_on(mixed, c, mixed_sent[c][0]).wait_recv()
        act_got[1, c] = expand(1, c)

    def contract_rows(s, c):
        here = pl.ds(c * PART, PART)
        return mm(act_own[s, here, :], dn_w[span(n * 1024, 1024), :]) + mm(
            act_o[s, here, :], dn_w[span((1 - n) * 1024, 1024), :]
        )

    rs2 = []
    for c in range(2):
        act_got[1, c].wait_recv()
        rs2.append(reduce_send(1, c, contract_rows(1, c)))
    for c in range(2):
        act_got[0, c].wait_recv()
        acc[pl.ds(c * PART, PART), :] = contract_rows(0, c)

    stats2 = []
    for c in range(2):
        rs2[c].wait_recv()

        def gather(i):
            rows = span(c * PART + i * STEP, STEP, 64)
            r = res1[rows, :] * gain1[...] + shift1[...]
            r = r + acc[rows, :] + rs_recv[1, rows, :].astype(F32) + dn_b[...]
            res2[rows, :] = r
            e = dy[rows, :].astype(F32) * gain2[...]
            stat_send[1, rows, :] = stat_pack(
                [row_sum(r), row_sum(r * r), row_sum(e), row_sum(e * r)]
            )

        tiles(PART // STEP, gather)
        stats2.append(stat_exchange(1, c))
    grad_down = (gd_own, gd_o)
    gd_sent = []
    for c in range(2):
        stats2[c].wait_recv()

        def normalize(i):
            rows = span(c * PART + i * STEP, STEP, 64)
            center = stat_total(1, rows, 0) / features
            inverse = lax.rsqrt(stat_total(1, rows, 1) / features - center * center + EPSILON)
            normed = (res2[rows, :] - center) * inverse
            hid_out[rows, :] = (normed * gain2[...] + shift2[...]).astype(BF)
            d = dy[rows, :].astype(F32)
            e = d * gain2[...]
            total = stat_total(1, rows, 2)
            cross = inverse * (stat_total(1, rows, 3) - center * total)
            grad = inverse * (e - total / features - normed * (cross / features))
            res2[rows, :] = grad
            gd_own[0, rows, :] = grad.astype(BF)
            column_add(SMALL_NORM + 4, d * normed)
            column_add(SMALL_NORM + 6, d)

        tiles(PART // STEP, normalize)
        gd_sent.append(spread(grad_down, c))

    dnw_got.wait_recv()

    def shrink_back(s, c):
        here = pl.ds(c * PART, PART)
        pre[...] = mm_right(gd_own[s, here, :], dn_w[span(n * 1024, 1024), :]) + mm_right(
            gd_o[s, here, :], dnw_o[...]
        )

        def bend(i):
            rows = span(i * 32, 32, 32)
            there = span(c * PART + i * 32, 32, 32)
            gu_own[s, there, :] = (pre[rows, :] * slope[s, there, :].astype(F32)).astype(BF)

        tiles(PART // 32, bend)
        return net.send(gu_own.at[s, here], gu_o.at[s, here], twin)

    gu_got = {}
    for c in range(2):
        gd_sent[c][1].wait_recv()
        gu_got[0, c] = shrink_back(0, c)
    for c in range(2):
        pass_on(grad_down, c, gd_sent[c][0]).wait_recv()
        gu_got[1, c] = shrink_back(1, c)

    def mixed_back(s, c):
        here = pl.ds(c * PART, PART)
        return mm_right(gu_own[s, here, :], up_w[:, span(n * 1024, 1024)]) + mm_right(
            gu_o[s, here, :], up_w[:, span((1 - n) * 1024, 1024)]
        )

    rs3 = []
    for c in range(2):
        gu_got[1, c].wait_recv()
        rs3.append(reduce_send(2, c, mixed_back(1, c)))
    for c in range(2):
        gu_got[0, c].wait_recv()
        acc[pl.ds(c * PART, PART), :] = mixed_back(0, c)

    def feed_forward_grads():
        for part, (a, g) in enumerate(((act_own, gu_own), (act_o, gu_o))):
            side = n if part == 0 else 1 - n

            def down_block(i):
                cols = span(i * 256, 256)
                got = mm_left(a[0, :, cols], gd_own[0]) + mm_left(a[1, :, cols], gd_own[1])
                packed[span(DOWN_BASE + side * 1024 + i * 256, 256), :] = got.astype(BF)

            tiles(4, down_block)

            def up_block(i):
                j, r = i % 2, i // 2
                cols, where = span(j * 512, 512), span(r * 256, 256)
                got = mm_left(mixed_own[0, :, where], g[0, :, cols]) + mm_left(
                    mixed_own[1, :, where], g[1, :, cols]
                )
                packed[span(UP_BASE + (side * 2 + j) * 512 + r * 256, 256), :] = got.astype(BF)

            tiles(4, up_block)

            def up_bias(i):
                cols = span(i * 256, 256)
                total = jnp.sum(g[0, :, cols].astype(F32), 0, keepdims=True) + jnp.sum(
                    g[1, :, cols].astype(F32), 0, keepdims=True
                )
                small[pl.ds(SMALL_UP + side * 4 + i, 1), :] = total

            tiles(4, up_bias)
        for s in range(2):
            column_add(SMALL_DOWN, gd_own[s].astype(F32))

    feed_forward_grads()

    stats3 = []
    for c in range(2):
        rs3[c].wait_recv()

        def gather(i):
            rows = span(c * PART + i * STEP, STEP, 64)
            g = res2[rows, :] + acc[rows, :] + rs_recv[2, rows, :].astype(F32)
            res2[rows, :] = g
            e = g * gain1[...]
            n1 = res1[rows, :]
            stat_send[2, rows, :] = stat_pack([row_sum(e), row_sum(e * n1)])
            column_add(SMALL_NORM, g * n1)
            column_add(SMALL_NORM + 2, g)

        tiles(PART // STEP, gather)
        stats3.append(stat_exchange(2, c))
    grad_attn = (ga_own, ga_o)
    ga_sent = []
    for c in range(2):
        stats3[c].wait_recv()

        def normalize(i):
            rows = span(c * PART + i * STEP, STEP, 64)
            e = res2[rows, :] * gain1[...]
            inverse = inv1[rows, 0:1]
            grad = inverse * (
                e
                - stat_total(2, rows, 0) / features
                - res1[rows, :] * (stat_total(2, rows, 1) / features)
            )
            res2[rows, :] = grad
            ga_own[0, rows, :] = grad.astype(BF)

        tiles(PART // STEP, normalize)
        ga_sent.append(spread(grad_attn, c))

    outw_got.wait_recv()

    def attend_back(s):
        dctx[...] = (
            mm_right(ga_own[s], out_w[span(n * 256, 256), :]) + mm_right(ga_o[s], outw_o[...])
        ).astype(BF)

        def block(p):
            q, k, v, d = qs[s, p], ks[s, p], vs[s, p], dctx[:, span(p * 128, 128)]
            dq, dk, dv = [], [], []
            for h in range(2):
                weight = probs[s, p * 2 + h]
                wide_weight = weight.astype(F32)
                dprob = mm_right(d * picks[h], v)
                inner = jnp.sum(dprob * wide_weight, -1, keepdims=True)
                dscore = (wide_weight * (dprob - inner)).astype(BF)
                dq.append(mm(dscore, k))
                dk.append(mm_left(dscore, q))
                dv.append(mm_left(weight, d))
            dqs = jnp.where(low, dq[0], dq[1]) * scale
            dks = pltpu.roll(jnp.where(low, dk[0], dk[1]) * scale, 64, 1)
            dvs = jnp.where(low, dv[0], dv[1])
            dqkv_own[s, :, span(p * 384, 128)] = jnp.where(low, dqs, dks).astype(BF)
            dqkv_own[s, :, span(p * 384 + 128, 128)] = jnp.where(low, dvs, dqs).astype(BF)
            dqkv_own[s, :, span(p * 384 + 256, 128)] = jnp.where(low, dks, dvs).astype(BF)

        tiles(2, block)
        return net.send(dqkv_own.at[s], dqkv_o.at[s], twin)

    for c in range(2):
        ga_sent[c][1].wait_recv()
    dqkv_got = [attend_back(0), None]
    ga_passed = [pass_on(grad_attn, c, ga_sent[c][0]) for c in range(2)]
    for copy in ga_passed:
        copy.wait_recv()
    dqkv_got[1] = attend_back(1)

    for part, ctx in enumerate((ctx_own, ctx_o)):
        side = n if part == 0 else 1 - n
        got = mm_left(ctx[0], ga_own[0]) + mm_left(ctx[1], ga_own[1])
        packed[span(OUT_BASE + side * 256, 256), :] = got.astype(BF)
    for s in range(2):
        column_add(SMALL_OUT, ga_own[s].astype(F32))

    def input_rows(s, c):
        here = pl.ds(c * PART, PART)
        return mm_right(dqkv_own[s, here, :], qkv_w[:, span(n * 768, 768)]) + mm_right(
            dqkv_o[s, here, :], qkv_w[:, span((1 - n) * 768, 768)]
        )

    dqkv_got[1].wait_recv()
    rs4 = [reduce_send(3, c, input_rows(1, c)) for c in range(2)]
    dqkv_got[0].wait_recv()
    for c in range(2):
        acc[pl.ds(c * PART, PART), :] = input_rows(0, c)

    for part, g in enumerate((dqkv_own, dqkv_o)):
        side = n if part == 0 else 1 - n

        def qkv_block(i):
            j, r = i // 2, i % 2
            cols, where = span(j * 256, 256), span(r * 256, 256)
            got = mm_left(hid[span(base_of[0], SEQ), where], g[0, :, cols]) + mm_left(
                hid[span(base_of[1], SEQ), where], g[1, :, cols]
            )
            at = side * 3 + j
            packed[
                span(QKV_BASE + (at // 2) * 512 + r * 256, 256), span((at % 2) * 256, 256)
            ] = got.astype(BF)

        tiles(6, qkv_block)

        def qkv_bias(j):
            cols = span(j * 256, 256)
            total = jnp.sum(g[0, :, cols].astype(F32), 0, keepdims=True) + jnp.sum(
                g[1, :, cols].astype(F32), 0, keepdims=True
            )
            small[pl.ds(SMALL_QKV + side * 3 + j, 1), :] = total

        tiles(3, qkv_bias)

    for c in range(2):
        rs4[c].wait_recv()

        def finish(i):
            rows = span(c * PART + i * STEP, STEP, 64)
            in_grad[rows, :] = res2[rows, :] + acc[rows, :] + rs_recv[3, rows, :].astype(F32)

        tiles(PART // STEP, finish)
    net.close()


def layer_call(*arrays):
    vmem = pl.BlockSpec(memory_space=pltpu.VMEM)
    shapes = [
        ((2, SEQ, 512), BF), ((512, 768), BF), ((256, 512), BF), ((512, 1024), BF), ((1024, 512), BF),
        ((2, 2, SEQ, 128), BF), ((2, 2, SEQ, 128), BF), ((2, 2, SEQ, 128), BF),
        ((2, 4, SEQ, SEQ), BF), ((2, SEQ, 256), BF), ((2, SEQ, 256), BF),
        ((4, SEQ, 512), BF), ((4, SEQ, 512), BF), ((3, SEQ, 128), F32), ((3, SEQ, 128), F32),
        ((SEQ, 512), F32), ((SEQ, 512), F32), ((SEQ, 512), F32), ((SEQ, 128), F32), ((PART, 1024), F32),
        ((2, SEQ, 512), BF), ((2, SEQ, 512), BF), ((2, SEQ, 1024), BF), ((2, SEQ, 1024), BF),
        ((2, SEQ, 1024), BF), ((2, SEQ, 512), BF), ((2, SEQ, 512), BF), ((2, SEQ, 1024), BF),
        ((2, SEQ, 1024), BF), ((2, SEQ, 512), BF), ((2, SEQ, 512), BF),
        ((SEQ, 256), BF), ((2, SEQ, 768), BF), ((2, SEQ, 768), BF),
    ]
    return pl.pallas_call(
        layer_kernel,
        out_shape=(
            jax.ShapeDtypeStruct((SEQ, 512), BF),
            jax.ShapeDtypeStruct((SEQ, 512), F32),
            jax.ShapeDtypeStruct((PACKED_ROWS, PACK), BF),
            jax.ShapeDtypeStruct((ROWS_SMALL, 256), F32),
        ),
        in_specs=[vmem] * len(arrays),
        out_specs=(vmem,) * 4,
        scratch_shapes=[pltpu.VMEM(*shape) for shape in shapes]
        + [pltpu.SemaphoreType.DMA((MESSAGES,)), pltpu.SemaphoreType.DMA((MESSAGES,))],
        compiler_params=pltpu.CompilerParams(
            collective_id=2, has_side_effects=True, vmem_limit_bytes=60 * 2**20
        ),
    )(*arrays)


def per_device(
    hidden_in,
    segment_ids,
    qkv_weight,
    qv_bias,
    out_weight,
    out_bias,
    norm1_gain,
    norm1_shift,
    up_weight,
    up_bias,
    down_weight,
    down_bias,
    norm2_gain,
    norm2_shift,
    out_grad,
):
    half_width = hidden_in.shape[1]
    heads_here, head_width = qkv_weight.shape[1], qkv_weight.shape[3]
    hidden_out, input_grad, packed, small = layer_call(
        hidden_in,
        segment_ids.reshape(2, SEQ),
        segment_ids.reshape(-1, 1),
        qkv_weight.reshape(half_width, -1),
        qv_bias.reshape(heads_here, -1),
        out_weight.reshape(-1, half_width),
        out_bias[None],
        norm1_gain[None],
        norm1_shift[None],
        up_weight,
        up_bias[None],
        down_weight,
        down_bias[None],
        norm2_gain[None],
        norm2_shift[None],
        out_grad,
    )
    total, small = sum_over_dp(packed, small)
    total = total.astype(F32)

    def columns(base, rows):
        return jnp.concatenate(
            [total[i : i + half_width] for i in range(base, base + rows, half_width)], 1
        )

    qkv_sums = small[SMALL_QKV : SMALL_QKV + 6].reshape(heads_here, 3, head_width)
    norms = small[SMALL_NORM : SMALL_NORM + 8].reshape(4, half_width)
    return (
        hidden_out,
        input_grad,
        columns(QKV_BASE, QKV_ROWS).reshape(half_width, heads_here, 3, head_width),
        jnp.stack([qkv_sums[:, 0], qkv_sums[:, 2]], 1),
        total[OUT_BASE : OUT_BASE + OUT_ROWS].reshape(heads_here, head_width, half_width),
        small[SMALL_OUT : SMALL_OUT + 2].reshape(-1),
        norms[0],
        norms[1],
        columns(UP_BASE, UP_ROWS),
        small[SMALL_UP : SMALL_UP + 8].reshape(-1),
        total[DOWN_BASE : DOWN_BASE + DOWN_ROWS],
        small[SMALL_DOWN : SMALL_DOWN + 2].reshape(-1),
        norms[2],
        norms[3],
    )


def solution(mesh):
    return jax.shard_map(
        per_device,
        mesh=mesh,
        in_specs=(
            P("dp", "narrow"),
            P("dp"),
            P("narrow", "wide", None, None),
            P("wide", None, None),
            P("wide", None, "narrow"),
            P("narrow"),
            P("narrow"),
            P("narrow"),
            P("narrow", "wide"),
            P("wide"),
            P("wide", "narrow"),
            P("narrow"),
            P("narrow"),
            P("narrow"),
            P(("dp", "wide"), "narrow"),
        ),
        out_specs=(
            P(("dp", "wide"), "narrow"),
            P(("dp", "wide"), "narrow"),
            P("narrow", "wide", None, None),
            P("wide", None, None),
            P("wide", None, "narrow"),
            P("narrow"),
            P("narrow"),
            P("narrow"),
            P("narrow", "wide"),
            P("wide"),
            P("wide", "narrow"),
            P("narrow"),
            P("narrow"),
            P("narrow"),
        ),
        check_vma=False,
    )
```

```python
import jax
import jax.numpy as jnp
from jax import lax
from jax.experimental import pallas as pl
from jax.experimental.pallas import tpu as pltpu
from jax.sharding import PartitionSpec as P

EPSILON = 1e-05
NEGATIVE = -1000000000.0
MESH = pl.DeviceIdType.MESH
BF = jnp.bfloat16
F32 = jnp.float32
PACK = 512


def partner_table():
    dp = lax.axis_index("dp")
    z, y, xh = dp // 8, (dp // 2) % 4, dp % 2
    wide, narrow = lax.axis_index("wide"), lax.axis_index("narrow")

    def at(z, y, xh):
        return (z * 8 + y * 2 + xh, wide, narrow)

    def parity(v):
        return (v % 2 + v // 2) % 2

    return {
        "y1": (at(z, y + 1 - 2 * (y % 2), xh), parity(y)),
        "z1": (at(z + 1 - 2 * (z % 2), y, xh), parity(z)),
        "y3": (at(z, 3 - y, xh), y // 2),
        "z3": (at(3 - z, y, xh), z // 2),
        "xh": (at(z, y, 1 - xh), xh),
        "wide": ((dp, 1 - wide, narrow), wide),
    }


ORDERS = (
    ("y1", "z1", "y3", "z3"),
    ("z1", "y3", "z3", "y1"),
    ("y3", "z3", "y1", "z1"),
    ("z3", "y1", "z1", "y3"),
)
SMALL_ORDER = ("wide", "y1", "z1", "y3", "z3", "xh")


class Summing:
    def __init__(self, buf, landing, fin, out, sems, base, rows, fin_base, table):
        self.buf, self.landing, self.fin, self.out = buf, landing, fin, out
        self.send_sem, self.recv_sem, self.local_sem = sems
        self.table, self.fin_base = table, fin_base
        self.quarter = rows // 4
        self.offsets, self.places = [], []
        for q, order in enumerate(ORDERS):
            offset, size, place = base + q * self.quarter, self.quarter, 0
            trail, slots = [offset], []
            for name in order:
                size = size // 2
                offset = pl.multiple_of(offset + table[name][1] * size, 16)
                trail.append(offset)
                slots.append(place)
                place += size
            slots.append(place)
            self.offsets.append(trail)
            self.places.append(slots)
        self.sent = []

    def size(self, level):
        return self.quarter >> level

    def final(self, q):
        return pl.ds(self.fin_base + q * self.size(4), self.size(4))

    def make(self, q, step):
        if step < 4:
            name, size = ORDERS[q][step], self.size(step + 1)
            start = self.offsets[q][step] + (1 - self.table[name][1]) * size
            src = self.buf.at[pl.ds(pl.multiple_of(start, 16), size), :]
            dst = self.landing(q, self.places[q][step], size)
        elif step == 4:
            name, size = "xh", self.size(4)
            src = self.buf.at[pl.ds(self.offsets[q][4], size), :]
            dst = self.landing(q, self.places[q][4], size)
        else:
            level = 9 - step
            name, size = ORDERS[q][level - 1], self.size(level)
            dst = self.out.at[pl.ds(self.offsets[q][level], size), :]
            src = self.fin.at[self.final(q), :] if step == 5 else dst
        return pltpu.make_async_remote_copy(
            src_ref=src,
            dst_ref=dst,
            send_sem=self.send_sem.at[q, step],
            recv_sem=self.recv_sem.at[q, step],
            device_id=self.table[name][0],
            device_id_type=MESH,
        )

    def keep(self, q):
        where = pl.ds(self.offsets[q][4], self.size(4))
        return pltpu.make_async_copy(
            self.fin.at[self.final(q), :], self.out.at[where, :], self.local_sem.at[q]
        )

    def begin(self, q, step):
        copy = self.make(q, step)
        copy.start()
        self.sent.append(copy)

    def take(self, q, step):
        self.make(q, step).wait_recv()
        if step > 4:
            return
        size, chunk = self.size(min(step + 1, 4)), 32
        offset, place = self.offsets[q][min(step + 1, 4)], self.places[q][step]

        def add(i, carry):
            here = pl.ds(pl.multiple_of(offset + i * chunk, 16), chunk)
            there = self.landing(q, pl.multiple_of(place + i * chunk, 16), chunk)
            total = (self.buf[here, :].astype(F32) + there[...].astype(F32)).astype(BF)
            if step == 4:
                first = self.fin_base + q * size
                self.fin[pl.ds(pl.multiple_of(first + i * chunk, 16), chunk), :] = total
            else:
                self.buf[here, :] = total
            return carry

        lax.fori_loop(0, size // chunk, add, 0)
        if step == 4:
            self.keep(q).start()

    def open(self):
        for q in range(4):
            self.begin(q, 0)

    def advance(self, step):
        for q in range(4):
            self.take(q, step)
            if step == 5:
                self.keep(q).wait()
            if step < 8:
                self.begin(q, step + 1)

    def close(self):
        for copy in self.sent:
            copy.wait_send()


class SmallSum:
    def __init__(self, held, kept, recv, sems, table):
        self.held, self.kept, self.recv, self.table = held, kept, recv, table
        self.send_sem, self.recv_sem = sems
        self.sent = []

    def begin(self, step):
        self.kept[step] = self.held[...]
        first = 24 if step == 0 else 0
        copy = pltpu.make_async_remote_copy(
            src_ref=self.kept.at[step, pl.ds(first, ROWS_SMALL - first)],
            dst_ref=self.recv.at[step, pl.ds(first, ROWS_SMALL - first)],
            send_sem=self.send_sem.at[step],
            recv_sem=self.recv_sem.at[step],
            device_id=self.table[SMALL_ORDER[step]][0],
            device_id_type=MESH,
        )
        copy.start()
        self.sent.append(copy)

    def take(self, step):
        self.sent[step].wait_recv()
        first = 24 if step == 0 else 0
        self.held[first:, :] = self.held[first:, :] + self.recv[step, first:, :]
        if step + 1 < len(SMALL_ORDER):
            self.begin(step + 1)

    def close(self):
        for copy in self.sent:
            copy.wait_send()


SEQ = 512
PART = 256
ROWS_SMALL = 32
SMALL_QKV, SMALL_UP, SMALL_OUT, SMALL_DOWN, SMALL_NORM = 0, 6, 14, 16, 24
HALF_ROOT = 0.7071067811865476
INV_ROOT_2PI = 0.3989422804014327
QKV_ROWS, OUT_ROWS, UP_ROWS, DOWN_ROWS = 1536, 512, 2048, 2048
PACKED_ROWS = QKV_ROWS + OUT_ROWS + UP_ROWS + DOWN_ROWS
UP_BASE, DOWN_BASE, QKV_BASE, OUT_BASE = 0, 2048, 4096, 5632


def mm(a, b):
    return lax.dot_general(a, b, (((1,), (0,)), ((), ())), preferred_element_type=F32)


def mm_right(a, b):
    return lax.dot_general(a, b, (((1,), (1,)), ((), ())), preferred_element_type=F32)


def mm_left(a, b):
    return lax.dot_general(a, b, (((0,), (0,)), ((), ())), preferred_element_type=F32)


def span(start, size, step=128):
    return pl.ds(pl.multiple_of(start, step), size)


def tiles(count, body):
    lax.fori_loop(0, count, lambda i, carry: (body(i), carry)[1], 0)


class Net:
    def __init__(self, send_sem, recv_sem):
        self.send_sem, self.recv_sem = send_sem, recv_sem
        self.sent, self.drained = [], []

    def send(self, src, dst, device):
        i = len(self.sent)
        copy = pltpu.make_async_remote_copy(
            src_ref=src,
            dst_ref=dst,
            send_sem=self.send_sem.at[i],
            recv_sem=self.recv_sem.at[i],
            device_id=device,
            device_id_type=MESH,
        )
        copy.start()
        self.sent.append(copy)
        return copy

    def drain(self, copies):
        for copy in copies:
            if not any(copy is done for done in self.drained):
                copy.wait_send()
                self.drained.append(copy)

    def close(self):
        self.drain(self.sent)


MESSAGES = 64


def layer_kernel(
    hid, seg, qkv_w, qv_b, out_w, out_b, gain1, shift1, up_w, up_b, dn_w, dn_b,
    gain2, shift2, dy,
    hid_out, in_grad, out, small,
    hid_o, qkvw_o, outw_o, upw_o, dnw_o,
    qs, ks, vs, probs, ctx_own, ctx_o,
    rs_send, rs_recv, stat_send, stat_recv,
    acc, res1, res2, inv1, pre,
    mixed_own, mixed_o, act_own, act_o, slope, gd_own, gd_o, gu_own, gu_o, ga_own, ga_o,
    dctx, packed, landing1, fin, small_kept, small_recv,
    send_sem, recv_sem, ss1, rs1_sem, ls1, ss2, rs2_sem, ls2, small_ss, small_rs,
):
    dp, w, n = lax.axis_index("dp"), lax.axis_index("wide"), lax.axis_index("narrow")
    twin, peer = (dp, w, 1 - n), (dp, 1 - w, n)
    table = partner_table()
    barrier = pltpu.get_barrier_semaphore()
    for device in [twin] + [entry[0] for entry in table.values()]:
        pl.semaphore_signal(barrier, inc=1, device_id=device, device_id_type=MESH)
    pl.semaphore_wait(barrier, 1 + len(table))
    net = Net(send_sem, recv_sem)
    seq_of = (w, 1 - w)
    base_of = (w * SEQ, (1 - w) * SEQ)
    lane = lax.broadcasted_iota(jnp.int32, (1, 128), 1)
    low = lane < 64
    picks = (low.astype(F32).astype(BF), (lane >= 64).astype(F32).astype(BF))
    scale = 0.125
    width = hid.shape[1]
    features = 2.0 * width

    hid_got = [None, None]
    hid_got[1] = net.send(hid.at[span(base_of[1], SEQ)], hid_o.at[1], twin)
    qkvw_got = net.send(qkv_w.at[:, span((1 - n) * 768, 768)], qkvw_o, twin)
    hid_got[0] = net.send(hid.at[span(base_of[0], SEQ)], hid_o.at[0], twin)
    upw_got = net.send(up_w.at[:, span((1 - n) * 1024, 1024)], upw_o, twin)
    dnw_got = net.send(dn_w.at[span((1 - n) * 1024, 1024), :], dnw_o, twin)
    outw_got = net.send(out_w.at[span((1 - n) * 256, 256), :], outw_o, twin)

    small[...] = jnp.zeros_like(small)

    def project(s):
        def block(i):
            p, r = i // 2, i % 2
            here = span(r * PART, PART)
            got = mm(hid[span(base_of[s] + r * PART, PART), :], qkv_w[:, span(n * 768 + p * 384, 384)])
            got += mm(hid_o[s, here, :], qkvw_o[:, span(p * 384, 384)])
            b0, b1, b2 = got[:, :128], got[:, 128:256], got[:, 256:]
            head = n * 4 + 2 * p
            q_bias, v_bias = [
                jnp.concatenate([qv_b[head, i : i + 1, :], qv_b[head + 1, i : i + 1, :]], 1)
                for i in range(2)
            ]
            qs[s, p, here, :] = (jnp.where(low, b0, b1) + q_bias).astype(BF)
            ks[s, p, here, :] = jnp.where(low, pltpu.roll(b0, 64, 1), pltpu.roll(b2, 64, 1)).astype(BF)
            vs[s, p, here, :] = (jnp.where(low, b1, b2) + v_bias).astype(BF)

        tiles(4, block)

    def segments(s):
        row = jnp.concatenate([seg[pl.ds(4 * seq_of[s] + i, 1), :] for i in range(4)], 1)
        row = row.astype(F32)
        return row, jnp.transpose(jnp.broadcast_to(row, (128, SEQ)))

    def attend_forward(s, r):
        here = pl.ds(r * PART, PART)
        row, column = segments(s)
        same = column[r * PART : (r + 1) * PART, 0:1] == row

        def block(p):
            q, k, v = qs[s, p, here, :], ks[s, p], vs[s, p]
            parts = []
            for h in range(2):
                score = jnp.where(same, mm_right(q * picks[h], k) * scale, NEGATIVE)
                raised = jnp.exp(score - jnp.max(score, -1, keepdims=True))
                weight = (raised / jnp.sum(raised, -1, keepdims=True)).astype(BF)
                probs[s, p * 2 + h, here, :] = weight
                parts.append(mm(weight, v))
            ctx_own[s, here, span(p * 128, 128)] = jnp.where(low, parts[0], parts[1]).astype(BF)

        tiles(2, block)
        return net.send(ctx_own.at[s, here], ctx_o.at[s, here], twin)

    def out_rows(s, c):
        here = pl.ds(c * PART, PART)
        return mm(ctx_own[s, here, :], out_w[span(n * 256, 256), :]) + mm(
            ctx_o[s, here, :], out_w[span((1 - n) * 256, 256), :]
        )

    rs_sent = {}

    def reduce_send(k, c, rows):
        here = pl.ds(c * PART, PART)
        slot = k % 2
        if k >= 2:
            net.drain([rs_sent[k - 2, c]])
        rs_send[slot, here, :] = rows.astype(BF)
        rs_sent[k, c] = net.send(rs_send.at[slot, here], rs_recv.at[slot, here], peer)

    def stat_pack(values):
        values = list(values) + [values[-1]] * (4 - len(values))
        return jnp.where(
            lane < 64,
            jnp.where(lane < 32, values[0], values[1]),
            jnp.where(lane < 96, values[2], values[3]),
        )

    def stat_exchange(k, c):
        here = pl.ds(c * PART, PART)
        return net.send(stat_send.at[k, here], stat_recv.at[k, here], twin)

    def stat_total(k, rows, i):
        return stat_send[k, rows, 32 * i : 32 * i + 1] + stat_recv[k, rows, 32 * i : 32 * i + 1]

    def row_sum(values):
        return jnp.sum(values, -1, keepdims=True)

    def column_add(row, values):
        for j in range(2):
            small[row + j : row + j + 1, :] += jnp.sum(
                values[:, j * 256 : (j + 1) * 256], 0, keepdims=True
            )

    STEP = 64

    def spread(own, c):
        here = pl.ds(c * PART, PART)
        across = net.send(own[0].at[0, here], own[0].at[1, here], peer)
        beside = net.send(own[0].at[0, here], own[1].at[0, here], twin)
        return across, beside

    def pass_on(own, c, across):
        here = pl.ds(c * PART, PART)
        across.wait_recv()
        return net.send(own[0].at[1, here], own[1].at[1, here], twin)

    hid_got[1].wait_recv()
    qkvw_got.wait_recv()
    project(1)
    ctx_got = {}
    for c in range(2):
        ctx_got[1, c] = attend_forward(1, c)
    ctx_got[1, 0].wait_recv()
    reduce_send(0, 0, out_rows(1, 0))
    hid_got[0].wait_recv()
    project(0)
    ctx_got[1, 1].wait_recv()
    reduce_send(0, 1, out_rows(1, 1))
    for c in range(2):
        ctx_got[0, c] = attend_forward(0, c)
    for c in range(2):
        ctx_got[0, c].wait_recv()
        acc[pl.ds(c * PART, PART), :] = out_rows(0, c)

    mixed = (mixed_own, mixed_o)
    mixed_sent = []
    for c in range(2):
        rs_sent[0, c].wait_recv()

        def gather(i):
            rows = span(c * PART + i * STEP, STEP, 64)
            r = hid[span(base_of[0] + c * PART + i * STEP, STEP, 64), :].astype(F32)
            r = r + acc[rows, :] + rs_recv[0, rows, :].astype(F32) + out_b[...]
            res1[rows, :] = r
            stat_send[0, rows, :] = stat_pack([row_sum(r), row_sum(r * r)])

        tiles(PART // STEP, gather)
        stat_exchange(0, c).wait_recv()

        def normalize(i):
            rows = span(c * PART + i * STEP, STEP, 64)
            center = stat_total(0, rows, 0) / features
            inverse = lax.rsqrt(stat_total(0, rows, 1) / features - center * center + EPSILON)
            normed = (res1[rows, :] - center) * inverse
            res1[rows, :] = normed
            inv1[rows, :] = jnp.broadcast_to(inverse, (STEP, 128))
            mixed_own[0, rows, :] = (normed * gain1[...] + shift1[...]).astype(BF)

        tiles(PART // STEP, normalize)
        mixed_sent.append(spread(mixed, c))

    upw_got.wait_recv()

    def expand(s, c):
        here = pl.ds(c * PART, PART)
        pre[...] = mm(mixed_own[s, here, :], up_w[:, span(n * 1024, 1024)]) + mm(
            mixed_o[s, here, :], upw_o[...]
        )

        def bend(i):
            rows = span(i * 32, 32, 32)
            there = span(c * PART + i * 32, 32, 32)
            u = pre[rows, :] + up_b[:, span(n * 1024, 1024)]
            share = 0.5 * (1.0 + lax.erf(u * HALF_ROOT))
            act_own[s, there, :] = (u * share).astype(BF)
            slope[s, there, :] = (share + u * (INV_ROOT_2PI * jnp.exp(-0.5 * u * u))).astype(BF)

        tiles(PART // 32, bend)
        return net.send(act_own.at[s, here], act_o.at[s, here], twin)

    def contract_rows(s, c):
        here = pl.ds(c * PART, PART)
        return mm(act_own[s, here, :], dn_w[span(n * 1024, 1024), :]) + mm(
            act_o[s, here, :], dn_w[span((1 - n) * 1024, 1024), :]
        )

    act_got = {}
    passed = []
    for c in range(2):
        mixed_sent[c][1].wait_recv()
        act_got[0, c] = expand(0, c)
        if c == 0:
            passed.append(pass_on(mixed, 0, mixed_sent[0][0]))
    passed[0].wait_recv()
    act_got[1, 0] = expand(1, 0)
    passed.append(pass_on(mixed, 1, mixed_sent[1][0]))
    act_got[0, 0].wait_recv()
    acc[pl.ds(0, PART), :] = contract_rows(0, 0)
    act_got[1, 0].wait_recv()
    reduce_send(1, 0, contract_rows(1, 0))
    passed[1].wait_recv()
    act_got[1, 1] = expand(1, 1)
    act_got[0, 1].wait_recv()
    acc[pl.ds(PART, PART), :] = contract_rows(0, 1)
    act_got[1, 1].wait_recv()
    reduce_send(1, 1, contract_rows(1, 1))

    grad_down = (gd_own, gd_o)
    gd_sent = []
    for c in range(2):
        rs_sent[1, c].wait_recv()

        def gather(i):
            rows = span(c * PART + i * STEP, STEP, 64)
            r = res1[rows, :] * gain1[...] + shift1[...]
            r = r + acc[rows, :] + rs_recv[1, rows, :].astype(F32) + dn_b[...]
            res2[rows, :] = r
            e = dy[rows, :].astype(F32) * gain2[...]
            stat_send[1, rows, :] = stat_pack(
                [row_sum(r), row_sum(r * r), row_sum(e), row_sum(e * r)]
            )

        tiles(PART // STEP, gather)
        stat_exchange(1, c).wait_recv()

        def normalize(i):
            rows = span(c * PART + i * STEP, STEP, 64)
            center = stat_total(1, rows, 0) / features
            inverse = lax.rsqrt(stat_total(1, rows, 1) / features - center * center + EPSILON)
            normed = (res2[rows, :] - center) * inverse
            hid_out[rows, :] = (normed * gain2[...] + shift2[...]).astype(BF)
            d = dy[rows, :].astype(F32)
            e = d * gain2[...]
            total = stat_total(1, rows, 2)
            cross = inverse * (stat_total(1, rows, 3) - center * total)
            grad = inverse * (e - total / features - normed * (cross / features))
            res2[rows, :] = grad
            gd_own[0, rows, :] = grad.astype(BF)
            column_add(SMALL_NORM + 4, d * normed)
            column_add(SMALL_NORM + 6, d)

        tiles(PART // STEP, normalize)
        gd_sent.append(spread(grad_down, c))

    dnw_got.wait_recv()

    def shrink_back(s, c):
        here = pl.ds(c * PART, PART)
        pre[...] = mm_right(gd_own[s, here, :], dn_w[span(n * 1024, 1024), :]) + mm_right(
            gd_o[s, here, :], dnw_o[...]
        )

        def bend(i):
            rows = span(i * 32, 32, 32)
            there = span(c * PART + i * 32, 32, 32)
            gu_own[s, there, :] = (pre[rows, :] * slope[s, there, :].astype(F32)).astype(BF)

        tiles(PART // 32, bend)
        return net.send(gu_own.at[s, here], gu_o.at[s, here], twin)

    def mixed_back(s, c):
        here = pl.ds(c * PART, PART)
        return mm_right(gu_own[s, here, :], up_w[:, span(n * 1024, 1024)]) + mm_right(
            gu_o[s, here, :], up_w[:, span((1 - n) * 1024, 1024)]
        )

    gu_got = {}
    passed = []
    for c in range(2):
        gd_sent[c][1].wait_recv()
        gu_got[0, c] = shrink_back(0, c)
        if c == 0:
            passed.append(pass_on(grad_down, 0, gd_sent[0][0]))
    passed[0].wait_recv()
    gu_got[1, 0] = shrink_back(1, 0)
    passed.append(pass_on(grad_down, 1, gd_sent[1][0]))
    gu_got[0, 0].wait_recv()
    acc[pl.ds(0, PART), :] = mixed_back(0, 0)
    gu_got[1, 0].wait_recv()
    reduce_send(2, 0, mixed_back(1, 0))
    passed[1].wait_recv()
    gu_got[1, 1] = shrink_back(1, 1)
    gu_got[0, 1].wait_recv()
    acc[pl.ds(PART, PART), :] = mixed_back(0, 1)
    gu_got[1, 1].wait_recv()
    reduce_send(2, 1, mixed_back(1, 1))

    def feed_forward_grads():
        for part, (a, g) in enumerate(((act_own, gu_own), (act_o, gu_o))):
            side = n if part == 0 else 1 - n

            def down_block(i):
                cols = span(i * 256, 256)
                got = mm_left(a[0, :, cols], gd_own[0]) + mm_left(a[1, :, cols], gd_own[1])
                packed[span(DOWN_BASE + side * 1024 + i * 256, 256), :] = got.astype(BF)

            tiles(4, down_block)

            def up_block(i):
                j, r = i % 2, i // 2
                cols, where = span(j * 512, 512), span(r * 256, 256)
                got = mm_left(mixed_own[0, :, where], g[0, :, cols]) + mm_left(
                    mixed_own[1, :, where], g[1, :, cols]
                )
                packed[span(UP_BASE + (side * 2 + j) * 512 + r * 256, 256), :] = got.astype(BF)

            tiles(4, up_block)

            def up_bias(i):
                cols = span(i * 256, 256)
                total = jnp.sum(g[0, :, cols].astype(F32), 0, keepdims=True) + jnp.sum(
                    g[1, :, cols].astype(F32), 0, keepdims=True
                )
                small[pl.ds(SMALL_UP + side * 4 + i, 1), :] = total

            tiles(4, up_bias)
        for s in range(2):
            column_add(SMALL_DOWN, gd_own[s].astype(F32))

    feed_forward_grads()
    sum1 = Summing(
        packed,
        lambda q, place, size: landing1.at[q, pl.ds(place, size), :],
        fin, out, (ss1, rs1_sem, ls1), 0, UP_ROWS + DOWN_ROWS, 0, table,
    )
    sum1.open()

    grad_attn = (ga_own, ga_o)
    ga_sent = []
    for c in range(2):
        rs_sent[2, c].wait_recv()

        def gather(i):
            rows = span(c * PART + i * STEP, STEP, 64)
            g = res2[rows, :] + acc[rows, :] + rs_recv[0, rows, :].astype(F32)
            res2[rows, :] = g
            e = g * gain1[...]
            n1 = res1[rows, :]
            stat_send[2, rows, :] = stat_pack([row_sum(e), row_sum(e * n1)])
            column_add(SMALL_NORM, g * n1)
            column_add(SMALL_NORM + 2, g)

        tiles(PART // STEP, gather)
        stat_exchange(2, c).wait_recv()

        def normalize(i):
            rows = span(c * PART + i * STEP, STEP, 64)
            e = res2[rows, :] * gain1[...]
            inverse = inv1[rows, 0:1]
            grad = inverse * (
                e
                - stat_total(2, rows, 0) / features
                - res1[rows, :] * (stat_total(2, rows, 1) / features)
            )
            res2[rows, :] = grad
            ga_own[0, rows, :] = grad.astype(BF)

        tiles(PART // STEP, normalize)
        ga_sent.append(spread(grad_attn, c))

    outw_got.wait_recv()

    def attend_back(s):
        dctx[...] = (
            mm_right(ga_own[s], out_w[span(n * 256, 256), :]) + mm_right(ga_o[s], outw_o[...])
        ).astype(BF)

        def block(p):
            q, k, v, d = qs[s, p], ks[s, p], vs[s, p], dctx[:, span(p * 128, 128)]
            dq, dk, dv = [], [], []
            for h in range(2):
                weight = probs[s, p * 2 + h]
                wide_weight = weight.astype(F32)
                dprob = mm_right(d * picks[h], v)
                inner = jnp.sum(dprob * wide_weight, -1, keepdims=True)
                dscore = (wide_weight * (dprob - inner)).astype(BF)
                dq.append(mm(dscore, k))
                dk.append(mm_left(dscore, q))
                dv.append(mm_left(weight, d))
            dqs = jnp.where(low, dq[0], dq[1]) * scale
            dks = pltpu.roll(jnp.where(low, dk[0], dk[1]) * scale, 64, 1)
            dvs = jnp.where(low, dv[0], dv[1])
            act_own[s, :, span(p * 384, 128)] = jnp.where(low, dqs, dks).astype(BF)
            act_own[s, :, span(p * 384 + 128, 128)] = jnp.where(low, dvs, dqs).astype(BF)
            act_own[s, :, span(p * 384 + 256, 128)] = jnp.where(low, dks, dvs).astype(BF)

        tiles(2, block)
        return net.send(act_own.at[s, :, pl.ds(0, 768)], slope.at[s, :, pl.ds(0, 768)], twin)

    net.drain(act_got.values())
    for c in range(2):
        ga_sent[c][1].wait_recv()
    dqkv_got = [attend_back(0), None]
    passed = [pass_on(grad_attn, c, ga_sent[c][0]) for c in range(2)]
    sum1.advance(0)
    for copy in passed:
        copy.wait_recv()
    dqkv_got[1] = attend_back(1)
    sum1.advance(1)

    for part, ctx in enumerate((ctx_own, ctx_o)):
        side = n if part == 0 else 1 - n
        got = mm_left(ctx[0], ga_own[0]) + mm_left(ctx[1], ga_own[1])
        packed[span(OUT_BASE + side * 256, 256), :] = got.astype(BF)
    for s in range(2):
        column_add(SMALL_OUT, ga_own[s].astype(F32))
    dqkv_got[0].wait_recv()
    dqkv_got[1].wait_recv()
    for part, g in enumerate((act_own, slope)):
        side = n if part == 0 else 1 - n

        def qkv_block(i):
            j, r = i // 2, i % 2
            cols, where = span(j * 256, 256), span(r * 256, 256)
            got = mm_left(hid[span(base_of[0], SEQ), where], g[0, :, cols]) + mm_left(
                hid[span(base_of[1], SEQ), where], g[1, :, cols]
            )
            at = side * 3 + j
            packed[
                span(QKV_BASE + (at // 2) * 512 + r * 256, 256), span((at % 2) * 256, 256)
            ] = got.astype(BF)

        tiles(6, qkv_block)

        def qkv_bias(j):
            cols = span(j * 256, 256)
            total = jnp.sum(g[0, :, cols].astype(F32), 0, keepdims=True) + jnp.sum(
                g[1, :, cols].astype(F32), 0, keepdims=True
            )
            small[pl.ds(SMALL_QKV + side * 3 + j, 1), :] = total

        tiles(3, qkv_bias)
    sum2 = Summing(
        packed,
        lambda q, place, size: act_o.at[q // 2, pl.ds(place, size), pl.ds((q % 2) * 512, 512)],
        fin, out, (ss2, rs2_sem, ls2), UP_ROWS + DOWN_ROWS, QKV_ROWS + OUT_ROWS, 256, table,
    )
    sum2.open()
    smalls = SmallSum(small, small_kept, small_recv, (small_ss, small_rs), table)
    smalls.begin(0)

    def input_rows(s, c):
        here = pl.ds(c * PART, PART)
        return mm_right(act_own[s, here, 0:768], qkv_w[:, span(n * 768, 768)]) + mm_right(
            slope[s, here, 0:768], qkv_w[:, span((1 - n) * 768, 768)]
        )

    for c in range(2):
        reduce_send(3, c, input_rows(1, c))
    sum1.advance(2)
    for c in range(2):
        acc[pl.ds(c * PART, PART), :] = input_rows(0, c)
    sum1.advance(3)
    sum2.advance(0)
    smalls.take(0)
    sum1.advance(4)
    sum2.advance(1)
    smalls.take(1)
    sum1.advance(5)
    for c in range(2):
        rs_sent[3, c].wait_recv()

        def finish(i):
            rows = span(c * PART + i * STEP, STEP, 64)
            in_grad[rows, :] = res2[rows, :] + acc[rows, :] + rs_recv[1, rows, :].astype(F32)

        tiles(PART // STEP, finish)
    for step in range(2, 9):
        sum2.advance(step)
        if step < 6:
            smalls.take(step)
        if step + 4 < 9:
            sum1.advance(step + 4)
    for work in (net, sum1, sum2, smalls):
        work.close()


def layer_call(*arrays):
    vmem = pl.BlockSpec(memory_space=pltpu.VMEM)
    shapes = [
        ((2, SEQ, 512), BF), ((512, 768), BF), ((256, 512), BF), ((512, 1024), BF), ((1024, 512), BF),
        ((2, 2, SEQ, 128), BF), ((2, 2, SEQ, 128), BF), ((2, 2, SEQ, 128), BF),
        ((2, 4, SEQ, SEQ), BF), ((2, SEQ, 256), BF), ((2, SEQ, 256), BF),
        ((2, SEQ, 512), BF), ((2, SEQ, 512), BF), ((3, SEQ, 128), F32), ((3, SEQ, 128), F32),
        ((SEQ, 512), F32), ((SEQ, 512), F32), ((SEQ, 512), F32), ((SEQ, 128), F32), ((PART, 1024), F32),
        ((2, SEQ, 512), BF), ((2, SEQ, 512), BF), ((2, SEQ, 1024), BF), ((2, SEQ, 1024), BF),
        ((2, SEQ, 1024), BF), ((2, SEQ, 512), BF), ((2, SEQ, 512), BF), ((2, SEQ, 1024), BF),
        ((2, SEQ, 1024), BF), ((2, SEQ, 512), BF), ((2, SEQ, 512), BF),
        ((SEQ, 256), BF), ((PACKED_ROWS, PACK), BF), ((4, 1024, PACK), BF), ((384, PACK), BF),
        ((6, ROWS_SMALL, 256), F32), ((6, ROWS_SMALL, 256), F32),
    ]
    return pl.pallas_call(
        layer_kernel,
        out_shape=(
            jax.ShapeDtypeStruct((SEQ, 512), BF),
            jax.ShapeDtypeStruct((SEQ, 512), F32),
            jax.ShapeDtypeStruct((PACKED_ROWS, PACK), BF),
            jax.ShapeDtypeStruct((ROWS_SMALL, 256), F32),
        ),
        in_specs=[vmem] * len(arrays),
        out_specs=(vmem, vmem, pl.BlockSpec(memory_space=pl.ANY), vmem),
        scratch_shapes=[pltpu.VMEM(*shape) for shape in shapes]
        + [
            pltpu.SemaphoreType.DMA(shape)
            for shape in (
                (MESSAGES,), (MESSAGES,), (4, 9), (4, 9), (4,), (4, 9), (4, 9), (4,), (6,), (6,)
            )
        ],
        compiler_params=pltpu.CompilerParams(
            collective_id=2, has_side_effects=True, vmem_limit_bytes=60 * 2**20
        ),
    )(*arrays)


def per_device(
    hidden_in,
    segment_ids,
    qkv_weight,
    qv_bias,
    out_weight,
    out_bias,
    norm1_gain,
    norm1_shift,
    up_weight,
    up_bias,
    down_weight,
    down_bias,
    norm2_gain,
    norm2_shift,
    out_grad,
):
    half_width = hidden_in.shape[1]
    heads_here, head_width = qkv_weight.shape[1], qkv_weight.shape[3]
    hidden_out, input_grad, total, small = layer_call(
        hidden_in,
        segment_ids.reshape(-1, 128),
        qkv_weight.reshape(half_width, -1),
        qv_bias,
        out_weight.reshape(-1, half_width),
        out_bias[None],
        norm1_gain[None],
        norm1_shift[None],
        up_weight,
        up_bias[None],
        down_weight,
        down_bias[None],
        norm2_gain[None],
        norm2_shift[None],
        out_grad,
    )

    def columns(base, rows):
        return jnp.concatenate(
            [total[i : i + half_width].astype(F32) for i in range(base, base + rows, half_width)], 1
        )

    qkv_sums = small[SMALL_QKV : SMALL_QKV + 6].reshape(heads_here, 3, head_width)
    norms = small[SMALL_NORM : SMALL_NORM + 8].reshape(4, half_width)
    return (
        hidden_out,
        input_grad,
        columns(QKV_BASE, QKV_ROWS).reshape(half_width, heads_here, 3, head_width),
        jnp.stack([qkv_sums[:, 0], qkv_sums[:, 2]], 1),
        total[OUT_BASE : OUT_BASE + OUT_ROWS].astype(F32).reshape(heads_here, head_width, half_width),
        small[SMALL_OUT : SMALL_OUT + 2].reshape(-1),
        norms[0],
        norms[1],
        columns(UP_BASE, UP_ROWS),
        small[SMALL_UP : SMALL_UP + 8].reshape(-1),
        total[DOWN_BASE : DOWN_BASE + DOWN_ROWS].astype(F32),
        small[SMALL_DOWN : SMALL_DOWN + 2].reshape(-1),
        norms[2],
        norms[3],
    )


def solution(mesh):
    return jax.shard_map(
        per_device,
        mesh=mesh,
        in_specs=(
            P("dp", "narrow"),
            P("dp"),
            P("narrow", "wide", None, None),
            P("wide", None, None),
            P("wide", None, "narrow"),
            P("narrow"),
            P("narrow"),
            P("narrow"),
            P("narrow", "wide"),
            P("wide"),
            P("wide", "narrow"),
            P("narrow"),
            P("narrow"),
            P("narrow"),
            P(("dp", "wide"), "narrow"),
        ),
        out_specs=(
            P(("dp", "wide"), "narrow"),
            P(("dp", "wide"), "narrow"),
            P("narrow", "wide", None, None),
            P("wide", None, None),
            P("wide", None, "narrow"),
            P("narrow"),
            P("narrow"),
            P("narrow"),
            P("narrow", "wide"),
            P("wide"),
            P("wide", "narrow"),
            P("narrow"),
            P("narrow"),
            P("narrow"),
        ),
        check_vma=False,
    )
```

```python
import jax
import jax.numpy as jnp
from jax import lax
from jax.experimental import pallas as pl
from jax.experimental.pallas import tpu as pltpu
from jax.sharding import PartitionSpec as P

EPSILON = 1e-05
NEGATIVE = -1000000000.0
MESH = pl.DeviceIdType.MESH
BF = jnp.bfloat16
F32 = jnp.float32
PACK = 512


def partner_table():
    dp = lax.axis_index("dp")
    z, y, xh = dp // 8, (dp // 2) % 4, dp % 2
    wide, narrow = lax.axis_index("wide"), lax.axis_index("narrow")

    def at(z, y, xh):
        return (z * 8 + y * 2 + xh, wide, narrow)

    def parity(v):
        return (v % 2 + v // 2) % 2

    return {
        "y1": (at(z, y + 1 - 2 * (y % 2), xh), parity(y)),
        "z1": (at(z + 1 - 2 * (z % 2), y, xh), parity(z)),
        "y3": (at(z, 3 - y, xh), y // 2),
        "z3": (at(3 - z, y, xh), z // 2),
        "xh": (at(z, y, 1 - xh), xh),
        "wide": ((dp, 1 - wide, narrow), wide),
    }


ORDERS = (
    ("y1", "z1", "y3", "z3"),
    ("z1", "y3", "z3", "y1"),
    ("y3", "z3", "y1", "z1"),
    ("z3", "y1", "z1", "y3"),
)
SMALL_ORDER = ("wide", "y1", "z1", "y3", "z3", "xh")


class Summing:
    def __init__(self, buf, landing, fin, out_at, sems, base, rows, fin_base, table):
        self.buf, self.landing, self.fin, self.out_at = buf, landing, fin, out_at
        self.send_sem, self.recv_sem, self.local_sem = sems
        self.table, self.fin_base = table, fin_base
        self.quarter = rows // 4
        self.offsets, self.places = [], []
        for q, order in enumerate(ORDERS):
            offset, size, place = base + q * self.quarter, self.quarter, 0
            trail, slots = [offset], []
            for name in order:
                size = size // 2
                offset = pl.multiple_of(offset + table[name][1] * size, 16)
                trail.append(offset)
                slots.append(place)
                place += size
            slots.append(place)
            self.offsets.append(trail)
            self.places.append(slots)
        self.sent = []

    def size(self, level):
        return self.quarter >> level

    def final(self, q):
        return pl.ds(self.fin_base + q * self.size(4), self.size(4))

    def make(self, q, step):
        if step < 4:
            name, size = ORDERS[q][step], self.size(step + 1)
            start = self.offsets[q][step] + (1 - self.table[name][1]) * size
            src = self.buf.at[pl.ds(pl.multiple_of(start, 16), size), :]
            dst = self.landing(q, self.places[q][step], size)
        elif step == 4:
            name, size = "xh", self.size(4)
            src = self.buf.at[pl.ds(self.offsets[q][4], size), :]
            dst = self.landing(q, self.places[q][4], size)
        else:
            level = 9 - step
            name, size = ORDERS[q][level - 1], self.size(level)
            dst = self.out_at(q, self.offsets[q][level], size)
            src = self.fin.at[self.final(q), :] if step == 5 else dst
        return pltpu.make_async_remote_copy(
            src_ref=src,
            dst_ref=dst,
            send_sem=self.send_sem.at[q, step],
            recv_sem=self.recv_sem.at[q, step],
            device_id=self.table[name][0],
            device_id_type=MESH,
        )

    def keep(self, q):
        where = self.out_at(q, self.offsets[q][4], self.size(4))
        return pltpu.make_async_copy(self.fin.at[self.final(q), :], where, self.local_sem.at[q])

    def begin(self, q, step):
        copy = self.make(q, step)
        copy.start()
        self.sent.append(copy)

    def take(self, q, step):
        self.make(q, step).wait_recv()
        if step > 4:
            return
        size, chunk = self.size(min(step + 1, 4)), 32
        offset, place = self.offsets[q][min(step + 1, 4)], self.places[q][step]

        def add(i, carry):
            here = pl.ds(pl.multiple_of(offset + i * chunk, 16), chunk)
            there = self.landing(q, pl.multiple_of(place + i * chunk, 16), chunk)
            total = (self.buf[here, :].astype(F32) + there[...].astype(F32)).astype(BF)
            if step == 4:
                first = self.fin_base + q * size
                self.fin[pl.ds(pl.multiple_of(first + i * chunk, 16), chunk), :] = total
            else:
                self.buf[here, :] = total
            return carry

        lax.fori_loop(0, size // chunk, add, 0)
        if step == 4:
            self.keep(q).start()

    def open(self):
        for q in range(4):
            self.begin(q, 0)

    def advance(self, step):
        for q in range(4):
            self.take(q, step)
            if step == 5:
                self.keep(q).wait()
            if step < 8:
                self.begin(q, step + 1)

    def close(self):
        for copy in self.sent:
            copy.wait_send()


class SmallSum:
    def __init__(self, held, kept, recv, sems, table):
        self.held, self.kept, self.recv, self.table = held, kept, recv, table
        self.send_sem, self.recv_sem = sems
        self.sent = []

    def begin(self, step):
        self.kept[step] = self.held[...]
        first = 24 if step == 0 else 0
        copy = pltpu.make_async_remote_copy(
            src_ref=self.kept.at[step, pl.ds(first, ROWS_SMALL - first)],
            dst_ref=self.recv.at[step, pl.ds(first, ROWS_SMALL - first)],
            send_sem=self.send_sem.at[step],
            recv_sem=self.recv_sem.at[step],
            device_id=self.table[SMALL_ORDER[step]][0],
            device_id_type=MESH,
        )
        copy.start()
        self.sent.append(copy)

    def take(self, step):
        self.sent[step].wait_recv()
        first = 24 if step == 0 else 0
        self.held[first:, :] = self.held[first:, :] + self.recv[step, first:, :]
        if step + 1 < len(SMALL_ORDER):
            self.begin(step + 1)

    def close(self):
        for copy in self.sent:
            copy.wait_send()


SEQ = 512
PART = 128
CHUNKS = SEQ // PART
HALF = 256
ROWS_SMALL = 32
SMALL_QKV, SMALL_UP, SMALL_OUT, SMALL_DOWN, SMALL_NORM = 0, 6, 14, 16, 24
HALF_ROOT = 0.7071067811865476
INV_ROOT_2PI = 0.3989422804014327
QKV_ROWS, OUT_ROWS, UP_ROWS, DOWN_ROWS = 1536, 512, 2048, 2048
PACKED_ROWS = QKV_ROWS + OUT_ROWS + UP_ROWS + DOWN_ROWS
UP_BASE, DOWN_BASE, QKV_BASE, OUT_BASE = 0, 2048, 4096, 5632


def mm(a, b):
    return lax.dot_general(a, b, (((1,), (0,)), ((), ())), preferred_element_type=F32)


def mm_right(a, b):
    return lax.dot_general(a, b, (((1,), (1,)), ((), ())), preferred_element_type=F32)


def mm_left(a, b):
    return lax.dot_general(a, b, (((0,), (0,)), ((), ())), preferred_element_type=F32)


def span(start, size, step=128):
    return pl.ds(pl.multiple_of(start, step), size)


def tiles(count, body):
    lax.fori_loop(0, count, lambda i, carry: (body(i), carry)[1], 0)


class Net:
    def __init__(self, send_sem, recv_sem):
        self.send_sem, self.recv_sem = send_sem, recv_sem
        self.sent, self.drained = [], []

    def send(self, src, dst, device):
        i = len(self.sent)
        copy = pltpu.make_async_remote_copy(
            src_ref=src,
            dst_ref=dst,
            send_sem=self.send_sem.at[i],
            recv_sem=self.recv_sem.at[i],
            device_id=device,
            device_id_type=MESH,
        )
        copy.start()
        self.sent.append(copy)
        return copy

    def drain(self, copies):
        for copy in copies:
            if not any(copy is done for done in self.drained):
                copy.wait_send()
                self.drained.append(copy)

    def close(self):
        self.drain(self.sent)


MESSAGES = 96


def layer_kernel(
    hid, seg, qkv_w, qv_b, out_src, out_b, gain1, shift1, up_src, up_b, dn_src, dn_b,
    gain2, shift2, dy_src,
    hid_out, in_grad, sum_qkv, sum_out, sum_up, sum_down, small,
    out_w, up_w, dn_w, dy, load_sem,
    hid_o, qkvw_o, outw_o, upw_o, dnw_o,
    qs, ks, vs, probs, ctx_own, ctx_o,
    rs_send, rs_recv, stat_send, stat_recv,
    acc, res1, res2, inv1, pre,
    mixed_own, mixed_o, act_own, act_o, slope, gd_own, gd_o, gu_own, gu_o, ga_own, ga_o,
    dctx, packed, landing1, fin, small_kept, small_recv,
    send_sem, recv_sem, ss1, rs1_sem, ls1, ss2, rs2_sem, ls2, small_ss, small_rs,
):
    dp, w, n = lax.axis_index("dp"), lax.axis_index("wide"), lax.axis_index("narrow")
    twin, peer = (dp, w, 1 - n), (dp, 1 - w, n)
    table = partner_table()
    loads = [
        pltpu.make_async_copy(src, dst, load_sem.at[i])
        for i, (src, dst) in enumerate(((out_src, out_w), (up_src, up_w), (dn_src, dn_w), (dy_src, dy)))
    ]
    for load in loads:
        load.start()
    barrier = pltpu.get_barrier_semaphore()
    for device in [twin] + [entry[0] for entry in table.values()]:
        pl.semaphore_signal(barrier, inc=1, device_id=device, device_id_type=MESH)
    pl.semaphore_wait(barrier, 1 + len(table))
    net = Net(send_sem, recv_sem)
    seq_of = (w, 1 - w)
    base_of = (w * SEQ, (1 - w) * SEQ)
    lane = lax.broadcasted_iota(jnp.int32, (1, 128), 1)
    low = lane < 64
    picks = (low.astype(F32).astype(BF), (lane >= 64).astype(F32).astype(BF))
    scale = 0.125
    width = hid.shape[1]
    features = 2.0 * width

    hid_got = [None, None]
    hid_got[1] = net.send(hid.at[span(base_of[1], SEQ)], hid_o.at[1], twin)
    qkvw_got = net.send(qkv_w.at[span((1 - n) * 768, 768), :], qkvw_o, twin)
    hid_got[0] = net.send(hid.at[span(base_of[0], SEQ)], hid_o.at[0], twin)

    small[...] = jnp.zeros_like(small)

    def project(s):
        def block(i):
            p, r = i // 2, i % 2
            here = span(r * HALF, HALF)
            mine = hid[span(base_of[s] + r * HALF, HALF), :]
            got = mm_right(mine, qkv_w[span(n * 768 + p * 384, 384), :])
            got += mm_right(hid_o[s, here, :], qkvw_o[span(p * 384, 384), :])
            b0, b1, b2 = got[:, :128], got[:, 128:256], got[:, 256:]
            head = n * 4 + 2 * p
            q_bias, v_bias = [
                jnp.concatenate([qv_b[head, i : i + 1, :], qv_b[head + 1, i : i + 1, :]], 1)
                for i in range(2)
            ]
            qs[s, p, here, :] = (jnp.where(low, b0, b1) + q_bias).astype(BF)
            ks[s, p, here, :] = jnp.where(low, pltpu.roll(b0, 64, 1), pltpu.roll(b2, 64, 1)).astype(BF)
            vs[s, p, here, :] = (jnp.where(low, b1, b2) + v_bias).astype(BF)

        tiles(4, block)

    def segments(s):
        row = jnp.concatenate([seg[pl.ds(4 * seq_of[s] + i, 1), :] for i in range(4)], 1)
        row = row.astype(F32)
        return row, jnp.transpose(jnp.broadcast_to(row, (128, SEQ)))

    def attend_forward(s, r):
        here = pl.ds(r * HALF, HALF)
        row, column = segments(s)
        same = column[r * HALF : (r + 1) * HALF, 0:1] == row

        def block(p):
            q, k, v = qs[s, p, here, :], ks[s, p], vs[s, p]
            parts = []
            for h in range(2):
                score = jnp.where(same, mm_right(q * picks[h], k) * scale, NEGATIVE)
                raised = jnp.exp(score - jnp.max(score, -1, keepdims=True))
                weight = (raised / jnp.sum(raised, -1, keepdims=True)).astype(BF)
                probs[s, p * 2 + h, here, :] = weight
                parts.append(mm(weight, v))
            ctx_own[s, here, span(p * 128, 128)] = jnp.where(low, parts[0], parts[1]).astype(BF)

        tiles(2, block)
        return net.send(ctx_own.at[s, here], ctx_o.at[s, here], twin)

    def out_rows(s, c):
        here = pl.ds(c * PART, PART)
        return mm(ctx_own[s, here, :], out_w[span(n * 256, 256), :]) + mm(
            ctx_o[s, here, :], out_w[span((1 - n) * 256, 256), :]
        )

    rs_sent = {}

    def two_way(pair, sent, first, second, k):
        passed, got = {}, {}

        def own(c):
            sent[c][1].wait_recv()
            got[0, c] = first(0, c)

        def hop(c):
            passed[c] = pass_on(pair, c, sent[c][0])

        def other(c):
            passed[c].wait_recv()
            got[1, c] = first(1, c)

        def push(c):
            got[1, c].wait_recv()
            reduce_send(k, c, second(1, c))

        own(0)
        for c in range(CHUNKS):
            if c + 1 < CHUNKS:
                own(c + 1)
            hop(c)
            if c >= 1:
                other(c - 1)
            if c >= 2:
                push(c - 2)
        other(CHUNKS - 1)
        push(CHUNKS - 2)
        push(CHUNKS - 1)
        for c in range(CHUNKS):
            got[0, c].wait_recv()
            acc[pl.ds(c * PART, PART), :] = second(0, c)
        return got

    def reduce_send(k, c, rows):
        here = pl.ds(c * PART, PART)
        slot = k % 2
        if k >= 2:
            net.drain([rs_sent[k - 2, c]])
        rs_send[slot, here, :] = rows.astype(BF)
        rs_sent[k, c] = net.send(rs_send.at[slot, here], rs_recv.at[slot, here], peer)

    def stat_pack(values):
        values = list(values) + [values[-1]] * (4 - len(values))
        return jnp.where(
            lane < 64,
            jnp.where(lane < 32, values[0], values[1]),
            jnp.where(lane < 96, values[2], values[3]),
        )

    def stat_exchange(k, c):
        here = pl.ds(c * PART, PART)
        return net.send(stat_send.at[k, here], stat_recv.at[k, here], twin)

    def stat_total(k, rows, i):
        return stat_send[k, rows, 32 * i : 32 * i + 1] + stat_recv[k, rows, 32 * i : 32 * i + 1]

    def row_sum(values):
        return jnp.sum(values, -1, keepdims=True)

    def column_add(row, values):
        for j in range(2):
            small[row + j : row + j + 1, :] += jnp.sum(
                values[:, j * 256 : (j + 1) * 256], 0, keepdims=True
            )

    STEP = 64

    def spread(own, c):
        here = pl.ds(c * PART, PART)
        across = net.send(own[0].at[0, here], own[0].at[1, here], peer)
        beside = net.send(own[0].at[0, here], own[1].at[0, here], twin)
        return across, beside

    def pass_on(own, c, across):
        here = pl.ds(c * PART, PART)
        across.wait_recv()
        return net.send(own[0].at[1, here], own[1].at[1, here], twin)

    hid_got[1].wait_recv()
    qkvw_got.wait_recv()
    project(1)
    ctx_got = {}
    for c in range(2):
        ctx_got[1, c] = attend_forward(1, c)
    upw_got = net.send(up_src.at[:, span((1 - n) * 1024, 1024)], upw_o, twin)
    loads[0].wait()
    ctx_got[1, 0].wait_recv()
    for c in range(CHUNKS // 2):
        reduce_send(0, c, out_rows(1, c))
    hid_got[0].wait_recv()
    project(0)
    ctx_got[1, 1].wait_recv()
    for c in range(CHUNKS // 2, CHUNKS):
        reduce_send(0, c, out_rows(1, c))
    for c in range(2):
        ctx_got[0, c] = attend_forward(0, c)
    for half in range(2):
        ctx_got[0, half].wait_recv()
        for c in range(half * CHUNKS // 2, (half + 1) * CHUNKS // 2):
            acc[pl.ds(c * PART, PART), :] = out_rows(0, c)

    mixed = (mixed_own, mixed_o)
    mixed_sent = []
    for c in range(CHUNKS):
        rs_sent[0, c].wait_recv()

        def gather(i):
            rows = span(c * PART + i * STEP, STEP, 64)
            r = hid[span(base_of[0] + c * PART + i * STEP, STEP, 64), :].astype(F32)
            r = r + acc[rows, :] + rs_recv[0, rows, :].astype(F32) + out_b[...]
            res1[rows, :] = r
            stat_send[0, rows, :] = stat_pack([row_sum(r), row_sum(r * r)])

        tiles(PART // STEP, gather)
        stat_exchange(0, c).wait_recv()

        def normalize(i):
            rows = span(c * PART + i * STEP, STEP, 64)
            center = stat_total(0, rows, 0) / features
            inverse = lax.rsqrt(stat_total(0, rows, 1) / features - center * center + EPSILON)
            normed = (res1[rows, :] - center) * inverse
            res1[rows, :] = normed
            inv1[rows, :] = jnp.broadcast_to(inverse, (STEP, 128))
            mixed_own[0, rows, :] = (normed * gain1[...] + shift1[...]).astype(BF)

        tiles(PART // STEP, normalize)
        mixed_sent.append(spread(mixed, c))

    dnw_got = net.send(dn_src.at[span((1 - n) * 1024, 1024), :], dnw_o, twin)
    loads[1].wait()
    upw_got.wait_recv()

    def expand(s, c):
        here = pl.ds(c * PART, PART)
        pre[...] = mm(mixed_own[s, here, :], up_w[:, span(n * 1024, 1024)]) + mm(
            mixed_o[s, here, :], upw_o[...]
        )

        def bend(i):
            rows = span(i * 32, 32, 32)
            there = span(c * PART + i * 32, 32, 32)
            u = pre[rows, :] + up_b[:, span(n * 1024, 1024)]
            share = 0.5 * (1.0 + lax.erf(u * HALF_ROOT))
            act_own[s, there, :] = (u * share).astype(BF)
            slope[s, there, :] = (share + u * (INV_ROOT_2PI * jnp.exp(-0.5 * u * u))).astype(BF)

        tiles(PART // 32, bend)
        return net.send(act_own.at[s, here], act_o.at[s, here], twin)

    def contract_rows(s, c):
        here = pl.ds(c * PART, PART)
        return mm(act_own[s, here, :], dn_w[span(n * 1024, 1024), :]) + mm(
            act_o[s, here, :], dn_w[span((1 - n) * 1024, 1024), :]
        )

    loads[2].wait()
    act_got = two_way(mixed, mixed_sent, expand, contract_rows, 1)

    outw_got = net.send(out_src.at[span((1 - n) * 256, 256), :], outw_o, twin)
    loads[3].wait()
    grad_down = (gd_own, gd_o)
    gd_sent = []
    for c in range(CHUNKS):
        rs_sent[1, c].wait_recv()

        def gather(i):
            rows = span(c * PART + i * STEP, STEP, 64)
            r = res1[rows, :] * gain1[...] + shift1[...]
            r = r + acc[rows, :] + rs_recv[1, rows, :].astype(F32) + dn_b[...]
            res2[rows, :] = r
            e = dy[rows, :].astype(F32) * gain2[...]
            stat_send[1, rows, :] = stat_pack(
                [row_sum(r), row_sum(r * r), row_sum(e), row_sum(e * r)]
            )

        tiles(PART // STEP, gather)
        stat_exchange(1, c).wait_recv()

        def normalize(i):
            rows = span(c * PART + i * STEP, STEP, 64)
            center = stat_total(1, rows, 0) / features
            inverse = lax.rsqrt(stat_total(1, rows, 1) / features - center * center + EPSILON)
            normed = (res2[rows, :] - center) * inverse
            hid_out[rows, :] = (normed * gain2[...] + shift2[...]).astype(BF)
            d = dy[rows, :].astype(F32)
            e = d * gain2[...]
            total = stat_total(1, rows, 2)
            cross = inverse * (stat_total(1, rows, 3) - center * total)
            grad = inverse * (e - total / features - normed * (cross / features))
            res2[rows, :] = grad
            gd_own[0, rows, :] = grad.astype(BF)
            column_add(SMALL_NORM + 4, d * normed)
            column_add(SMALL_NORM + 6, d)

        tiles(PART // STEP, normalize)
        gd_sent.append(spread(grad_down, c))

    dnw_got.wait_recv()

    def shrink_back(s, c):
        here = pl.ds(c * PART, PART)
        pre[...] = mm_right(gd_own[s, here, :], dn_w[span(n * 1024, 1024), :]) + mm_right(
            gd_o[s, here, :], dnw_o[...]
        )

        def bend(i):
            rows = span(i * 32, 32, 32)
            there = span(c * PART + i * 32, 32, 32)
            gu_own[s, there, :] = (pre[rows, :] * slope[s, there, :].astype(F32)).astype(BF)

        tiles(PART // 32, bend)
        return net.send(gu_own.at[s, here], gu_o.at[s, here], twin)

    def mixed_back(s, c):
        here = pl.ds(c * PART, PART)
        return mm_right(gu_own[s, here, :], up_w[:, span(n * 1024, 1024)]) + mm_right(
            gu_o[s, here, :], up_w[:, span((1 - n) * 1024, 1024)]
        )

    two_way(grad_down, gd_sent, shrink_back, mixed_back, 2)

    def feed_forward_grads():
        for part, (a, g) in enumerate(((act_own, gu_own), (act_o, gu_o))):
            side = n if part == 0 else 1 - n

            def down_block(i):
                cols = span(i * 256, 256)
                got = mm_left(a[0, :, cols], gd_own[0]) + mm_left(a[1, :, cols], gd_own[1])
                packed[span(DOWN_BASE + side * 1024 + i * 256, 256), :] = got.astype(BF)

            tiles(4, down_block)

            def up_block(i):
                j, r = i % 2, i // 2
                cols, where = span(j * 512, 512), span(r * 256, 256)
                got = mm_left(mixed_own[0, :, where], g[0, :, cols]) + mm_left(
                    mixed_own[1, :, where], g[1, :, cols]
                )
                packed[span(UP_BASE + (side * 2 + j) * 512 + r * 256, 256), :] = got.astype(BF)

            tiles(4, up_block)

            def up_bias(i):
                cols = span(i * 256, 256)
                total = jnp.sum(g[0, :, cols].astype(F32), 0, keepdims=True) + jnp.sum(
                    g[1, :, cols].astype(F32), 0, keepdims=True
                )
                small[pl.ds(SMALL_UP + side * 4 + i, 1), :] = total

            tiles(4, up_bias)
        for s in range(2):
            column_add(SMALL_DOWN, gd_own[s].astype(F32))

    feed_forward_grads()

    def feed_forward_out(q, start, size):
        if q < 2:
            return sum_up.at[
                pl.ds(pl.multiple_of(start % 512, 16), size), span(start // 512 * 512, 512)
            ]
        return sum_down.at[pl.ds(pl.multiple_of(start - DOWN_BASE, 16), size), :]

    def attention_out(q, start, size):
        if q < 3:
            return sum_qkv.at[pl.ds(pl.multiple_of(start - QKV_BASE, 16), size), :]
        return sum_out.at[pl.ds(pl.multiple_of(start - OUT_BASE, 16), size), :]

    sum1 = Summing(
        packed,
        lambda q, place, size: landing1.at[q, pl.ds(place, size), :],
        fin, feed_forward_out, (ss1, rs1_sem, ls1), 0, UP_ROWS + DOWN_ROWS, 0, table,
    )
    sum1.open()

    grad_attn = (ga_own, ga_o)
    ga_sent = []
    for c in range(CHUNKS):
        rs_sent[2, c].wait_recv()

        def gather(i):
            rows = span(c * PART + i * STEP, STEP, 64)
            g = res2[rows, :] + acc[rows, :] + rs_recv[0, rows, :].astype(F32)
            res2[rows, :] = g
            e = g * gain1[...]
            n1 = res1[rows, :]
            stat_send[2, rows, :] = stat_pack([row_sum(e), row_sum(e * n1)])
            column_add(SMALL_NORM, g * n1)
            column_add(SMALL_NORM + 2, g)

        tiles(PART // STEP, gather)
        stat_exchange(2, c).wait_recv()

        def normalize(i):
            rows = span(c * PART + i * STEP, STEP, 64)
            e = res2[rows, :] * gain1[...]
            inverse = inv1[rows, 0:1]
            grad = inverse * (
                e
                - stat_total(2, rows, 0) / features
                - res1[rows, :] * (stat_total(2, rows, 1) / features)
            )
            res2[rows, :] = grad
            ga_own[0, rows, :] = grad.astype(BF)

        tiles(PART // STEP, normalize)
        ga_sent.append(spread(grad_attn, c))

    outw_got.wait_recv()

    def context_back(s):
        dctx[...] = (
            mm_right(ga_own[s], out_w[span(n * 256, 256), :]) + mm_right(ga_o[s], outw_o[...])
        ).astype(BF)

    def back_pair(s, p):
        q, k, v, d = qs[s, p], ks[s, p], vs[s, p], dctx[:, span(p * 128, 128)]
        dq, dk, dv = [], [], []
        for h in range(2):
            weight = probs[s, p * 2 + h]
            wide_weight = weight.astype(F32)
            dprob = mm_right(d * picks[h], v)
            inner = jnp.sum(dprob * wide_weight, -1, keepdims=True)
            dscore = (wide_weight * (dprob - inner)).astype(BF)
            dq.append(mm(dscore, k))
            dk.append(mm_left(dscore, q))
            dv.append(mm_left(weight, d))
        dqs = jnp.where(low, dq[0], dq[1]) * scale
        dks = pltpu.roll(jnp.where(low, dk[0], dk[1]) * scale, 64, 1)
        dvs = jnp.where(low, dv[0], dv[1])
        act_own[s, :, span(p * 384, 128)] = jnp.where(low, dqs, dks).astype(BF)
        act_own[s, :, span(p * 384 + 128, 128)] = jnp.where(low, dvs, dqs).astype(BF)
        act_own[s, :, span(p * 384 + 256, 128)] = jnp.where(low, dks, dvs).astype(BF)

    def send_qkv(s):
        return net.send(act_own.at[s, :, pl.ds(0, 768)], slope.at[s, :, pl.ds(0, 768)], twin)

    net.drain(act_got.values())
    for c in range(CHUNKS):
        ga_sent[c][1].wait_recv()
    sum1.advance(0)
    context_back(0)
    back_pair(0, 0)
    back_pair(0, 1)
    dqkv_got = [send_qkv(0)]
    passed = [pass_on(grad_attn, c, ga_sent[c][0]) for c in range(CHUNKS)]
    sum1.advance(1)
    for copy in passed:
        copy.wait_recv()
    context_back(1)
    back_pair(1, 0)
    back_pair(1, 1)
    dqkv_got.append(send_qkv(1))
    sum1.advance(2)

    for part, ctx in enumerate((ctx_own, ctx_o)):
        side = n if part == 0 else 1 - n
        got = mm_left(ctx[0], ga_own[0]) + mm_left(ctx[1], ga_own[1])
        packed[span(OUT_BASE + side * 256, 256), :] = got.astype(BF)
    for s in range(2):
        column_add(SMALL_OUT, ga_own[s].astype(F32))
    dqkv_got[0].wait_recv()
    dqkv_got[1].wait_recv()
    for part, g in enumerate((act_own, slope)):
        side = n if part == 0 else 1 - n

        def qkv_block(j):
            cols = span(j * 256, 256)
            got = mm_left(g[0, :, cols], hid[span(base_of[0], SEQ), :]) + mm_left(
                g[1, :, cols], hid[span(base_of[1], SEQ), :]
            )
            packed[span(QKV_BASE + side * 768 + j * 256, 256), :] = got.astype(BF)

        tiles(3, qkv_block)

        def qkv_bias(j):
            cols = span(j * 256, 256)
            total = jnp.sum(g[0, :, cols].astype(F32), 0, keepdims=True) + jnp.sum(
                g[1, :, cols].astype(F32), 0, keepdims=True
            )
            small[pl.ds(SMALL_QKV + side * 3 + j, 1), :] = total

        tiles(3, qkv_bias)
    sum2 = Summing(
        packed,
        lambda q, place, size: act_o.at[q // 2, pl.ds(place, size), pl.ds((q % 2) * 512, 512)],
        fin, attention_out, (ss2, rs2_sem, ls2), UP_ROWS + DOWN_ROWS, QKV_ROWS + OUT_ROWS, 256, table,
    )
    sum2.open()
    smalls = SmallSum(small, small_kept, small_recv, (small_ss, small_rs), table)
    smalls.begin(0)

    def input_rows(s, c):
        here = pl.ds(c * PART, PART)
        return mm(act_own[s, here, 0:768], qkv_w[span(n * 768, 768), :]) + mm(
            slope[s, here, 0:768], qkv_w[span((1 - n) * 768, 768), :]
        )

    sum1.advance(3)
    for c in range(CHUNKS):
        reduce_send(3, c, input_rows(1, c))
    for c in range(CHUNKS):
        acc[pl.ds(c * PART, PART), :] = input_rows(0, c)
    smalls.take(0)
    sum2.advance(0)
    sum1.advance(4)
    smalls.take(1)
    sum2.advance(1)
    sum1.advance(5)
    sum2.advance(2)
    smalls.take(2)
    for c in range(CHUNKS):
        rs_sent[3, c].wait_recv()

        def finish(i):
            rows = span(c * PART + i * STEP, STEP, 64)
            in_grad[rows, :] = res2[rows, :] + acc[rows, :] + rs_recv[1, rows, :].astype(F32)

        tiles(PART // STEP, finish)
    sum1.advance(6)
    sum2.advance(3)
    smalls.take(3)
    sum2.advance(4)
    smalls.take(4)
    sum2.advance(5)
    sum1.advance(7)
    smalls.take(5)
    sum2.advance(6)
    sum2.advance(7)
    sum1.advance(8)
    sum2.advance(8)
    for work in (net, sum1, sum2, smalls):
        work.close()


def layer_call(*arrays):
    vmem = pl.BlockSpec(memory_space=pltpu.VMEM)
    anywhere = pl.BlockSpec(memory_space=pl.ANY)
    shapes = [
        ((2, SEQ, 512), BF), ((768, 512), BF), ((256, 512), BF), ((512, 1024), BF), ((1024, 512), BF),
        ((2, 2, SEQ, 128), BF), ((2, 2, SEQ, 128), BF), ((2, 2, SEQ, 128), BF),
        ((2, 4, SEQ, SEQ), BF), ((2, SEQ, 256), BF), ((2, SEQ, 256), BF),
        ((2, SEQ, 512), BF), ((2, SEQ, 512), BF), ((3, SEQ, 128), F32), ((3, SEQ, 128), F32),
        ((SEQ, 512), F32), ((SEQ, 512), F32), ((SEQ, 512), F32), ((SEQ, 128), F32), ((PART, 1024), F32),
        ((2, SEQ, 512), BF), ((2, SEQ, 512), BF), ((2, SEQ, 1024), BF), ((2, SEQ, 1024), BF),
        ((2, SEQ, 1024), BF), ((2, SEQ, 512), BF), ((2, SEQ, 512), BF), ((2, SEQ, 1024), BF),
        ((2, SEQ, 1024), BF), ((2, SEQ, 512), BF), ((2, SEQ, 512), BF),
        ((SEQ, 256), BF), ((PACKED_ROWS, PACK), BF), ((4, 1024, PACK), BF), ((384, PACK), BF),
        ((6, ROWS_SMALL, 256), F32), ((6, ROWS_SMALL, 256), F32),
    ]
    return pl.pallas_call(
        layer_kernel,
        out_shape=(
            jax.ShapeDtypeStruct((SEQ, 512), BF),
            jax.ShapeDtypeStruct((SEQ, 512), F32),
            jax.ShapeDtypeStruct((QKV_ROWS, PACK), BF),
            jax.ShapeDtypeStruct((OUT_ROWS, PACK), BF),
            jax.ShapeDtypeStruct((512, UP_ROWS), BF),
            jax.ShapeDtypeStruct((DOWN_ROWS, PACK), BF),
            jax.ShapeDtypeStruct((ROWS_SMALL, 256), F32),
        ),
        in_specs=[anywhere if i in (4, 8, 10, 14) else vmem for i in range(len(arrays))],
        out_specs=(vmem, vmem) + (anywhere,) * 4 + (vmem,),
        scratch_shapes=[
            pltpu.VMEM((512, 512), BF),
            pltpu.VMEM((512, 2048), BF),
            pltpu.VMEM((2048, 512), BF),
            pltpu.VMEM((512, 512), BF),
            pltpu.SemaphoreType.DMA((4,)),
        ]
        + [pltpu.VMEM(*shape) for shape in shapes]
        + [
            pltpu.SemaphoreType.DMA(shape)
            for shape in (
                (MESSAGES,), (MESSAGES,), (4, 9), (4, 9), (4,), (4, 9), (4, 9), (4,), (6,), (6,)
            )
        ],
        compiler_params=pltpu.CompilerParams(
            collective_id=2, has_side_effects=True, vmem_limit_bytes=60 * 2**20
        ),
    )(*arrays)


def finish_kernel(
    hidden, grad, qkv, out, up, down, small,
    hidden_o, grad_o, qkv_o, out_o, up_o, down_o, qvb_o, outb_o, upb_o, downb_o, g1_o, s1_o, g2_o, s2_o,
):
    hidden_o[...] = hidden[...]
    grad_o[...] = grad[...]
    qkv_o[...] = qkv[...].astype(F32)
    out_o[...] = out[...].astype(F32)
    up_o[...] = up[...].astype(F32)
    down_o[...] = down[...].astype(F32)

    @pl.when(pl.program_id(0) == 0)
    def _():
        for head in range(8):
            for i in range(2):
                row, lane = divmod(head * 192 + i * 128, 256)
                row += SMALL_QKV
                qvb_o[head, i : i + 1, :] = small[row : row + 1, lane : lane + 64]
        bases = [SMALL_NORM + 2 * i for i in range(4)]
        for ref, first, count in (
            (outb_o, SMALL_OUT, 2),
            (upb_o, SMALL_UP, 8),
            (downb_o, SMALL_DOWN, 2),
            (g1_o, bases[0], 2),
            (s1_o, bases[1], 2),
            (g2_o, bases[2], 2),
            (s2_o, bases[3], 2),
        ):
            for j in range(count):
                ref[:, j * 256 : (j + 1) * 256] = small[first + j : first + j + 1, :]


def finish_call(hidden, grad, qkv, out, up, down, small):
    steps = 8

    def rows(shape):
        return pl.BlockSpec((shape[0] // steps, shape[1]), lambda i: (i, 0))

    def whole(shape):
        return pl.BlockSpec(shape, lambda i: (0,) * len(shape))

    big = [hidden, grad, qkv, out, up, down]
    thin = [(8, 2, 64), (1, 512), (1, 2048), (1, 512)] + [(1, 512)] * 4
    return pl.pallas_call(
        finish_kernel,
        grid=(steps,),
        out_shape=[
            jax.ShapeDtypeStruct(a.shape, BF if a is hidden else F32) for a in big
        ]
        + [jax.ShapeDtypeStruct(shape, F32) for shape in thin],
        in_specs=[rows(a.shape) for a in big] + [whole(small.shape)],
        out_specs=[rows(a.shape) for a in big] + [whole(shape) for shape in thin],
        compiler_params=pltpu.CompilerParams(vmem_limit_bytes=60 * 2**20),
    )(*big, small)


def per_device(
    hidden_in,
    segment_ids,
    qkv_weight,
    qv_bias,
    out_weight,
    out_bias,
    norm1_gain,
    norm1_shift,
    up_weight,
    up_bias,
    down_weight,
    down_bias,
    norm2_gain,
    norm2_shift,
    out_grad,
):
    half_width = hidden_in.shape[1]
    heads_here, head_width = qkv_weight.shape[1], qkv_weight.shape[3]
    results = layer_call(
        hidden_in,
        segment_ids.reshape(-1, 128),
        qkv_weight.transpose(1, 2, 3, 0).reshape(-1, half_width),
        qv_bias,
        out_weight.reshape(-1, half_width),
        out_bias[None],
        norm1_gain[None],
        norm1_shift[None],
        up_weight,
        up_bias[None],
        down_weight,
        down_bias[None],
        norm2_gain[None],
        norm2_shift[None],
        out_grad,
    )

    hidden_out, input_grad, qkv, out, up, down, qv, outb, upb, downb, *norms = finish_call(*results)
    return (
        hidden_out,
        input_grad,
        qkv.reshape(heads_here, 3, head_width, half_width).transpose(3, 0, 1, 2),
        qv,
        out.reshape(heads_here, head_width, half_width),
        outb.reshape(-1),
        norms[0].reshape(-1),
        norms[1].reshape(-1),
        up,
        upb.reshape(-1),
        down,
        downb.reshape(-1),
        norms[2].reshape(-1),
        norms[3].reshape(-1),
    )


def solution(mesh):
    return jax.shard_map(
        per_device,
        mesh=mesh,
        in_specs=(
            P("dp", "narrow"),
            P("dp"),
            P("narrow", "wide", None, None),
            P("wide", None, None),
            P("wide", None, "narrow"),
            P("narrow"),
            P("narrow"),
            P("narrow"),
            P("narrow", "wide"),
            P("wide"),
            P("wide", "narrow"),
            P("narrow"),
            P("narrow"),
            P("narrow"),
            P(("dp", "wide"), "narrow"),
        ),
        out_specs=(
            P(("dp", "wide"), "narrow"),
            P(("dp", "wide"), "narrow"),
            P("narrow", "wide", None, None),
            P("wide", None, None),
            P("wide", None, "narrow"),
            P("narrow"),
            P("narrow"),
            P("narrow"),
            P("narrow", "wide"),
            P("wide"),
            P("wide", "narrow"),
            P("narrow"),
            P("narrow"),
            P("narrow"),
        ),
        check_vma=False,
    )
```

```python
import jax
import jax.numpy as jnp
from jax import lax
from jax.experimental import pallas as pl
from jax.experimental.pallas import tpu as pltpu
from jax.sharding import PartitionSpec as P

EPSILON = 1e-05
NEGATIVE = -1000000000.0
MESH = pl.DeviceIdType.MESH
BF = jnp.bfloat16
F32 = jnp.float32
PACK = 512


def partner_table():
    dp = lax.axis_index("dp")
    z, y, xh = dp // 8, (dp // 2) % 4, dp % 2
    wide, narrow = lax.axis_index("wide"), lax.axis_index("narrow")

    def at(z, y, xh):
        return (z * 8 + y * 2 + xh, wide, narrow)

    def parity(v):
        return (v % 2 + v // 2) % 2

    return {
        "y1": (at(z, y + 1 - 2 * (y % 2), xh), parity(y)),
        "z1": (at(z + 1 - 2 * (z % 2), y, xh), parity(z)),
        "y3": (at(z, 3 - y, xh), y // 2),
        "z3": (at(3 - z, y, xh), z // 2),
        "xh": (at(z, y, 1 - xh), xh),
        "wide": ((dp, 1 - wide, narrow), wide),
    }


ORDERS = (
    ("y1", "z1", "y3", "z3"),
    ("z1", "y3", "z3", "y1"),
    ("y3", "z3", "y1", "z1"),
    ("z3", "y1", "z1", "y3"),
)
SMALL_ORDER = ("wide", "y1", "z1", "y3", "z3", "xh")


class Summing:
    def __init__(self, buf, landing, fin, out_at, sems, base, rows, fin_base, table):
        self.buf, self.landing, self.fin, self.out_at = buf, landing, fin, out_at
        self.send_sem, self.recv_sem, self.local_sem = sems
        self.table, self.fin_base = table, fin_base
        self.quarter = rows // 4
        self.offsets, self.places = [], []
        for q, order in enumerate(ORDERS):
            offset, size, place = base + q * self.quarter, self.quarter, 0
            trail, slots = [offset], []
            for name in order:
                size = size // 2
                offset = pl.multiple_of(offset + table[name][1] * size, 16)
                trail.append(offset)
                slots.append(place)
                place += size
            slots.append(place)
            self.offsets.append(trail)
            self.places.append(slots)
        self.sent = []

    def size(self, level):
        return self.quarter >> level

    def final(self, q):
        return pl.ds(self.fin_base + q * self.size(4), self.size(4))

    def make(self, q, step):
        if step < 4:
            name, size = ORDERS[q][step], self.size(step + 1)
            start = self.offsets[q][step] + (1 - self.table[name][1]) * size
            src = self.buf.at[pl.ds(pl.multiple_of(start, 16), size), :]
            dst = self.landing(q, self.places[q][step], size)
        elif step == 4:
            name, size = "xh", self.size(4)
            src = self.buf.at[pl.ds(self.offsets[q][4], size), :]
            dst = self.landing(q, self.places[q][4], size)
        else:
            level = 9 - step
            name, size = ORDERS[q][level - 1], self.size(level)
            dst = self.out_at(q, self.offsets[q][level], size)
            src = self.fin.at[self.final(q), :] if step == 5 else dst
        return pltpu.make_async_remote_copy(
            src_ref=src,
            dst_ref=dst,
            send_sem=self.send_sem.at[q, step],
            recv_sem=self.recv_sem.at[q, step],
            device_id=self.table[name][0],
            device_id_type=MESH,
        )

    def keep(self, q):
        where = self.out_at(q, self.offsets[q][4], self.size(4))
        return pltpu.make_async_copy(self.fin.at[self.final(q), :], where, self.local_sem.at[q])

    def begin(self, q, step):
        copy = self.make(q, step)
        copy.start()
        self.sent.append(copy)

    def take(self, q, step):
        self.make(q, step).wait_recv()
        if step > 4:
            return
        size = self.size(min(step + 1, 4))
        chunk = min(size, 64)
        offset, place = self.offsets[q][min(step + 1, 4)], self.places[q][step]

        def add(i, carry):
            here = pl.ds(pl.multiple_of(offset + i * chunk, 16), chunk)
            there = self.landing(q, pl.multiple_of(place + i * chunk, 16), chunk)
            total = self.buf[here, :] + there[...]
            if step == 4:
                first = self.fin_base + q * size
                self.fin[pl.ds(pl.multiple_of(first + i * chunk, 16), chunk), :] = total
            else:
                self.buf[here, :] = total
            return carry

        lax.fori_loop(0, size // chunk, add, 0)
        if step == 4:
            self.keep(q).start()

    def open(self):
        for q in range(4):
            self.begin(q, 0)

    def advance(self, step):
        for q in range(4):
            self.take(q, step)
            if step == 5:
                self.keep(q).wait()
            if step < 8:
                self.begin(q, step + 1)

    def close(self):
        for copy in self.sent:
            copy.wait_send()


class SmallSum:
    def __init__(self, held, kept, recv, sems, table):
        self.held, self.kept, self.recv, self.table = held, kept, recv, table
        self.send_sem, self.recv_sem = sems
        self.sent = []

    def begin(self, step):
        self.kept[step] = self.held[...]
        first = 24 if step == 0 else 0
        copy = pltpu.make_async_remote_copy(
            src_ref=self.kept.at[step, pl.ds(first, ROWS_SMALL - first)],
            dst_ref=self.recv.at[step, pl.ds(first, ROWS_SMALL - first)],
            send_sem=self.send_sem.at[step],
            recv_sem=self.recv_sem.at[step],
            device_id=self.table[SMALL_ORDER[step]][0],
            device_id_type=MESH,
        )
        copy.start()
        self.sent.append(copy)

    def take(self, step):
        self.sent[step].wait_recv()
        first = 24 if step == 0 else 0
        self.held[first:, :] = self.held[first:, :] + self.recv[step, first:, :]
        if step + 1 < len(SMALL_ORDER):
            self.begin(step + 1)

    def close(self):
        for copy in self.sent:
            copy.wait_send()


SEQ = 512
PART = 128
CHUNKS = SEQ // PART
HALF = 256
ROWS_SMALL = 32
SMALL_QKV, SMALL_UP, SMALL_OUT, SMALL_DOWN, SMALL_NORM = 0, 6, 14, 16, 24
HALF_ROOT = 0.7071067811865476
INV_ROOT_2PI = 0.3989422804014327
QKV_ROWS, OUT_ROWS, UP_ROWS, DOWN_ROWS = 1536, 512, 2048, 2048
PACKED_ROWS = QKV_ROWS + OUT_ROWS + UP_ROWS + DOWN_ROWS
UP_BASE, DOWN_BASE, QKV_BASE, OUT_BASE = 0, 2048, 4096, 5632


def mm(a, b):
    return lax.dot_general(a, b, (((1,), (0,)), ((), ())), preferred_element_type=F32)


def mm_right(a, b):
    return lax.dot_general(a, b, (((1,), (1,)), ((), ())), preferred_element_type=F32)


def mm_left(a, b):
    return lax.dot_general(a, b, (((0,), (0,)), ((), ())), preferred_element_type=F32)


def span(start, size, step=128):
    return pl.ds(pl.multiple_of(start, step), size)


def tiles(count, body):
    lax.fori_loop(0, count, lambda i, carry: (body(i), carry)[1], 0)


class Net:
    def __init__(self, send_sem, recv_sem):
        self.send_sem, self.recv_sem = send_sem, recv_sem
        self.sent, self.drained = [], []

    def send(self, src, dst, device):
        i = len(self.sent)
        copy = pltpu.make_async_remote_copy(
            src_ref=src,
            dst_ref=dst,
            send_sem=self.send_sem.at[i],
            recv_sem=self.recv_sem.at[i],
            device_id=device,
            device_id_type=MESH,
        )
        copy.start()
        self.sent.append(copy)
        return copy

    def drain(self, copies):
        for copy in copies:
            if not any(copy is done for done in self.drained):
                copy.wait_send()
                self.drained.append(copy)

    def close(self):
        self.drain(self.sent)


MESSAGES = 96


def layer_kernel(
    hid, seg, qkv_w, qv_b, out_src, out_b, gain1, shift1, up_src, up_b, dn_src, dn_b,
    gain2, shift2, dy_src,
    hid_out, in_grad, sum_qkv, sum_out, sum_up, sum_down, small,
    out_w, up_w, dn_w, dy, load_sem,
    hid_o, qkvw_o, outw_o, upw_o, dnw_o,
    qs, ks, vs, probs, ctx_own, ctx_o,
    rs_send, rs_recv, stat_send, stat_recv,
    acc, res1, res2, inv1, pre,
    mixed_own, mixed_o, act_own, act_o, slope, gd_own, gd_o, gu_own, gu_o, ga_own, ga_o,
    dctx, packed, landing1, fin, small_kept, small_recv,
    send_sem, recv_sem, ss1, rs1_sem, ls1, ss2, rs2_sem, ls2, small_ss, small_rs,
):
    dp, w, n = lax.axis_index("dp"), lax.axis_index("wide"), lax.axis_index("narrow")
    twin, peer = (dp, w, 1 - n), (dp, 1 - w, n)
    table = partner_table()
    loads = [
        pltpu.make_async_copy(src, dst, load_sem.at[i])
        for i, (src, dst) in enumerate(((out_src, out_w), (up_src, up_w), (dn_src, dn_w), (dy_src, dy)))
    ]
    for load in loads:
        load.start()
    barrier = pltpu.get_barrier_semaphore()
    for device in [twin] + [entry[0] for entry in table.values()]:
        pl.semaphore_signal(barrier, inc=1, device_id=device, device_id_type=MESH)
    pl.semaphore_wait(barrier, 1 + len(table))
    net = Net(send_sem, recv_sem)
    seq_of = (w, 1 - w)
    base_of = (w * SEQ, (1 - w) * SEQ)
    lane = lax.broadcasted_iota(jnp.int32, (1, 128), 1)
    low = lane < 64
    picks = (low.astype(F32).astype(BF), (lane >= 64).astype(F32).astype(BF))
    scale = 0.125
    width = hid.shape[1]
    features = 2.0 * width

    hid_got = [None, None]
    hid_got[1] = net.send(hid.at[span(base_of[1], SEQ)], hid_o.at[1], twin)
    qkvw_got = net.send(qkv_w.at[span((1 - n) * 768, 768), :], qkvw_o, twin)
    hid_got[0] = net.send(hid.at[span(base_of[0], SEQ)], hid_o.at[0], twin)

    small[...] = jnp.zeros_like(small)

    def project(s):
        def block(i):
            p, r = i // 2, i % 2
            here = span(r * HALF, HALF)
            mine = hid[span(base_of[s] + r * HALF, HALF), :]
            got = mm_right(mine, qkv_w[span(n * 768 + p * 384, 384), :])
            got += mm_right(hid_o[s, here, :], qkvw_o[span(p * 384, 384), :])
            b0, b1, b2 = got[:, :128], got[:, 128:256], got[:, 256:]
            head = n * 4 + 2 * p
            q_bias, v_bias = [
                jnp.concatenate([qv_b[head, i : i + 1, :], qv_b[head + 1, i : i + 1, :]], 1)
                for i in range(2)
            ]
            qs[s, p, here, :] = (jnp.where(low, b0, b1) + q_bias).astype(BF)
            ks[s, p, here, :] = jnp.where(low, pltpu.roll(b0, 64, 1), pltpu.roll(b2, 64, 1)).astype(BF)
            vs[s, p, here, :] = (jnp.where(low, b1, b2) + v_bias).astype(BF)

        tiles(4, block)

    def segments(s):
        row = jnp.concatenate([seg[pl.ds(4 * seq_of[s] + i, 1), :] for i in range(4)], 1)
        row = row.astype(F32)
        return row, jnp.transpose(jnp.broadcast_to(row, (128, SEQ)))

    def attend_forward(s, r):
        here = pl.ds(r * HALF, HALF)
        row, column = segments(s)
        same = column[r * HALF : (r + 1) * HALF, 0:1] == row

        def block(p):
            q, k, v = qs[s, p, here, :], ks[s, p], vs[s, p]
            parts = []
            for h in range(2):
                score = jnp.where(same, mm_right(q * picks[h], k) * scale, NEGATIVE)
                raised = jnp.exp(score - jnp.max(score, -1, keepdims=True))
                weight = (raised / jnp.sum(raised, -1, keepdims=True)).astype(BF)
                probs[s, p * 2 + h, here, :] = weight
                parts.append(mm(weight, v))
            ctx_own[s, here, span(p * 128, 128)] = jnp.where(low, parts[0], parts[1]).astype(BF)

        tiles(2, block)
        return net.send(ctx_own.at[s, here], ctx_o.at[s, here], twin)

    def out_rows(s, c):
        here = pl.ds(c * PART, PART)
        return mm(ctx_own[s, here, :], out_w[span(n * 256, 256), :]) + mm(
            ctx_o[s, here, :], out_w[span((1 - n) * 256, 256), :]
        )

    rs_sent = {}

    def two_way(pair, sent, first, second, k):
        passed, got = {}, {}

        def own(c):
            sent[c][1].wait_recv()
            got[0, c] = first(0, c)

        def hop(c):
            passed[c] = pass_on(pair, c, sent[c][0])

        def other(c):
            passed[c].wait_recv()
            got[1, c] = first(1, c)

        def push(c):
            got[1, c].wait_recv()
            reduce_send(k, c, second(1, c))

        own(0)
        for c in range(CHUNKS):
            if c + 1 < CHUNKS:
                own(c + 1)
            hop(c)
            if c >= 1:
                other(c - 1)
            if c >= 2:
                push(c - 2)
        other(CHUNKS - 1)
        push(CHUNKS - 2)
        push(CHUNKS - 1)
        for c in range(CHUNKS):
            got[0, c].wait_recv()
            acc[pl.ds(c * PART, PART), :] = second(0, c)
        return got

    def reduce_send(k, c, rows):
        here = pl.ds(c * PART, PART)
        slot = k % 2
        if k >= 2:
            net.drain([rs_sent[k - 2, c]])
        rs_send[slot, here, :] = rows.astype(BF)
        rs_sent[k, c] = net.send(rs_send.at[slot, here], rs_recv.at[slot, here], peer)

    def stat_pack(values):
        values = list(values) + [values[-1]] * (4 - len(values))
        return jnp.where(
            lane < 64,
            jnp.where(lane < 32, values[0], values[1]),
            jnp.where(lane < 96, values[2], values[3]),
        )

    def stat_exchange(k, c):
        here = pl.ds(c * PART, PART)
        return net.send(stat_send.at[k, here], stat_recv.at[k, here], twin)

    def stat_total(k, rows, i):
        return stat_send[k, rows, 32 * i : 32 * i + 1] + stat_recv[k, rows, 32 * i : 32 * i + 1]

    def row_sum(values):
        return jnp.sum(values, -1, keepdims=True)

    def column_add(row, values):
        for j in range(2):
            small[row + j : row + j + 1, :] += jnp.sum(
                values[:, j * 256 : (j + 1) * 256], 0, keepdims=True
            )

    STEP = 64

    def spread(own, c):
        here = pl.ds(c * PART, PART)
        across = net.send(own[0].at[0, here], own[0].at[1, here], peer)
        beside = net.send(own[0].at[0, here], own[1].at[0, here], twin)
        return across, beside

    def pass_on(own, c, across):
        here = pl.ds(c * PART, PART)
        across.wait_recv()
        return net.send(own[0].at[1, here], own[1].at[1, here], twin)

    hid_got[1].wait_recv()
    qkvw_got.wait_recv()
    project(1)
    ctx_got = {}
    for c in range(2):
        ctx_got[1, c] = attend_forward(1, c)
    upw_got = net.send(up_src.at[:, span((1 - n) * 1024, 1024)], upw_o, twin)
    loads[0].wait()
    ctx_got[1, 0].wait_recv()
    for c in range(CHUNKS // 2):
        reduce_send(0, c, out_rows(1, c))
    hid_got[0].wait_recv()
    project(0)
    ctx_got[1, 1].wait_recv()
    for c in range(CHUNKS // 2, CHUNKS):
        reduce_send(0, c, out_rows(1, c))
    for c in range(2):
        ctx_got[0, c] = attend_forward(0, c)
    for half in range(2):
        ctx_got[0, half].wait_recv()
        for c in range(half * CHUNKS // 2, (half + 1) * CHUNKS // 2):
            acc[pl.ds(c * PART, PART), :] = out_rows(0, c)

    mixed = (mixed_own, mixed_o)
    mixed_sent = []
    for c in range(CHUNKS):
        rs_sent[0, c].wait_recv()

        def gather(i):
            rows = span(c * PART + i * STEP, STEP, 64)
            r = hid[span(base_of[0] + c * PART + i * STEP, STEP, 64), :].astype(F32)
            r = r + acc[rows, :] + rs_recv[0, rows, :].astype(F32) + out_b[...]
            res1[rows, :] = r
            stat_send[0, rows, :] = stat_pack([row_sum(r), row_sum(r * r)])

        tiles(PART // STEP, gather)
        stat_exchange(0, c).wait_recv()

        def normalize(i):
            rows = span(c * PART + i * STEP, STEP, 64)
            center = stat_total(0, rows, 0) / features
            inverse = lax.rsqrt(stat_total(0, rows, 1) / features - center * center + EPSILON)
            normed = (res1[rows, :] - center) * inverse
            res1[rows, :] = normed
            inv1[rows, :] = jnp.broadcast_to(inverse, (STEP, 128))
            mixed_own[0, rows, :] = (normed * gain1[...] + shift1[...]).astype(BF)

        tiles(PART // STEP, normalize)
        mixed_sent.append(spread(mixed, c))

    dnw_got = net.send(dn_src.at[span((1 - n) * 1024, 1024), :], dnw_o, twin)
    loads[1].wait()
    upw_got.wait_recv()

    def expand(s, c):
        here = pl.ds(c * PART, PART)
        pre[...] = mm(mixed_own[s, here, :], up_w[:, span(n * 1024, 1024)]) + mm(
            mixed_o[s, here, :], upw_o[...]
        )

        def bend(i):
            rows = span(i * 32, 32, 32)
            there = span(c * PART + i * 32, 32, 32)
            u = pre[rows, :] + up_b[:, span(n * 1024, 1024)]
            share = 0.5 * (1.0 + lax.erf(u * HALF_ROOT))
            act_own[s, there, :] = (u * share).astype(BF)
            slope[s, there, :] = (share + u * (INV_ROOT_2PI * jnp.exp(-0.5 * u * u))).astype(BF)

        tiles(PART // 32, bend)
        return net.send(act_own.at[s, here], act_o.at[s, here], twin)

    def contract_rows(s, c):
        here = pl.ds(c * PART, PART)
        return mm(act_own[s, here, :], dn_w[span(n * 1024, 1024), :]) + mm(
            act_o[s, here, :], dn_w[span((1 - n) * 1024, 1024), :]
        )

    loads[2].wait()
    act_got = two_way(mixed, mixed_sent, expand, contract_rows, 1)

    outw_got = net.send(out_src.at[span((1 - n) * 256, 256), :], outw_o, twin)
    loads[3].wait()
    grad_down = (gd_own, gd_o)
    gd_sent = []
    for c in range(CHUNKS):
        rs_sent[1, c].wait_recv()

        def gather(i):
            rows = span(c * PART + i * STEP, STEP, 64)
            r = res1[rows, :] * gain1[...] + shift1[...]
            r = r + acc[rows, :] + rs_recv[1, rows, :].astype(F32) + dn_b[...]
            res2[rows, :] = r
            e = dy[rows, :].astype(F32) * gain2[...]
            stat_send[1, rows, :] = stat_pack(
                [row_sum(r), row_sum(r * r), row_sum(e), row_sum(e * r)]
            )

        tiles(PART // STEP, gather)
        stat_exchange(1, c).wait_recv()

        def normalize(i):
            rows = span(c * PART + i * STEP, STEP, 64)
            center = stat_total(1, rows, 0) / features
            inverse = lax.rsqrt(stat_total(1, rows, 1) / features - center * center + EPSILON)
            normed = (res2[rows, :] - center) * inverse
            hid_out[rows, :] = (normed * gain2[...] + shift2[...]).astype(BF)
            d = dy[rows, :].astype(F32)
            e = d * gain2[...]
            total = stat_total(1, rows, 2)
            cross = inverse * (stat_total(1, rows, 3) - center * total)
            grad = inverse * (e - total / features - normed * (cross / features))
            res2[rows, :] = grad
            gd_own[0, rows, :] = grad.astype(BF)
            column_add(SMALL_NORM + 4, d * normed)
            column_add(SMALL_NORM + 6, d)

        tiles(PART // STEP, normalize)
        gd_sent.append(spread(grad_down, c))

    dnw_got.wait_recv()

    def shrink_back(s, c):
        here = pl.ds(c * PART, PART)
        pre[...] = mm_right(gd_own[s, here, :], dn_w[span(n * 1024, 1024), :]) + mm_right(
            gd_o[s, here, :], dnw_o[...]
        )

        def bend(i):
            rows = span(i * 32, 32, 32)
            there = span(c * PART + i * 32, 32, 32)
            gu_own[s, there, :] = (pre[rows, :] * slope[s, there, :].astype(F32)).astype(BF)

        tiles(PART // 32, bend)
        return net.send(gu_own.at[s, here], gu_o.at[s, here], twin)

    def mixed_back(s, c):
        here = pl.ds(c * PART, PART)
        return mm_right(gu_own[s, here, :], up_w[:, span(n * 1024, 1024)]) + mm_right(
            gu_o[s, here, :], up_w[:, span((1 - n) * 1024, 1024)]
        )

    two_way(grad_down, gd_sent, shrink_back, mixed_back, 2)

    def feed_forward_grads():
        for part, (a, g) in enumerate(((act_own, gu_own), (act_o, gu_o))):
            side = n if part == 0 else 1 - n

            def down_block(i):
                cols = span(i * 256, 256)
                got = mm_left(a[0, :, cols], gd_own[0]) + mm_left(a[1, :, cols], gd_own[1])
                packed[span(DOWN_BASE + side * 1024 + i * 256, 256), :] = got.astype(BF)

            tiles(4, down_block)

            def up_block(i):
                j, r = i % 2, i // 2
                cols, where = span(j * 512, 512), span(r * 256, 256)
                got = mm_left(mixed_own[0, :, where], g[0, :, cols]) + mm_left(
                    mixed_own[1, :, where], g[1, :, cols]
                )
                packed[span(UP_BASE + (side * 2 + j) * 512 + r * 256, 256), :] = got.astype(BF)

            tiles(4, up_block)

            def up_bias(i):
                cols = span(i * 256, 256)
                total = jnp.sum(g[0, :, cols].astype(F32), 0, keepdims=True) + jnp.sum(
                    g[1, :, cols].astype(F32), 0, keepdims=True
                )
                small[pl.ds(SMALL_UP + side * 4 + i, 1), :] = total

            tiles(4, up_bias)
        for s in range(2):
            column_add(SMALL_DOWN, gd_own[s].astype(F32))

    feed_forward_grads()

    def feed_forward_out(q, start, size):
        if q < 2:
            return sum_up.at[
                pl.ds(pl.multiple_of(start % 512, 16), size), span(start // 512 * 512, 512)
            ]
        return sum_down.at[pl.ds(pl.multiple_of(start - DOWN_BASE, 16), size), :]

    def attention_out(q, start, size):
        if q < 3:
            return sum_qkv.at[pl.ds(pl.multiple_of(start - QKV_BASE, 16), size), :]
        return sum_out.at[pl.ds(pl.multiple_of(start - OUT_BASE, 16), size), :]

    sum1 = Summing(
        packed,
        lambda q, place, size: landing1.at[q, pl.ds(place, size), :],
        fin, feed_forward_out, (ss1, rs1_sem, ls1), 0, UP_ROWS + DOWN_ROWS, 0, table,
    )
    sum1.open()

    grad_attn = (ga_own, ga_o)
    ga_sent = []
    for c in range(CHUNKS):
        rs_sent[2, c].wait_recv()

        def gather(i):
            rows = span(c * PART + i * STEP, STEP, 64)
            g = res2[rows, :] + acc[rows, :] + rs_recv[0, rows, :].astype(F32)
            res2[rows, :] = g
            e = g * gain1[...]
            n1 = res1[rows, :]
            stat_send[2, rows, :] = stat_pack([row_sum(e), row_sum(e * n1)])
            column_add(SMALL_NORM, g * n1)
            column_add(SMALL_NORM + 2, g)

        tiles(PART // STEP, gather)
        stat_exchange(2, c).wait_recv()

        def normalize(i):
            rows = span(c * PART + i * STEP, STEP, 64)
            e = res2[rows, :] * gain1[...]
            inverse = inv1[rows, 0:1]
            grad = inverse * (
                e
                - stat_total(2, rows, 0) / features
                - res1[rows, :] * (stat_total(2, rows, 1) / features)
            )
            res2[rows, :] = grad
            ga_own[0, rows, :] = grad.astype(BF)

        tiles(PART // STEP, normalize)
        ga_sent.append(spread(grad_attn, c))

    outw_got.wait_recv()

    def context_back(s):
        dctx[...] = (
            mm_right(ga_own[s], out_w[span(n * 256, 256), :]) + mm_right(ga_o[s], outw_o[...])
        ).astype(BF)

    def back_pair(s, p):
        q, k, v, d = qs[s, p], ks[s, p], vs[s, p], dctx[:, span(p * 128, 128)]
        dq, dk, dv = [], [], []
        for h in range(2):
            weight = probs[s, p * 2 + h]
            wide_weight = weight.astype(F32)
            dprob = mm_right(d * picks[h], v)
            inner = jnp.sum(dprob * wide_weight, -1, keepdims=True)
            dscore = (wide_weight * (dprob - inner)).astype(BF)
            dq.append(mm(dscore, k))
            dk.append(mm_left(dscore, q))
            dv.append(mm_left(weight, d))
        dqs = jnp.where(low, dq[0], dq[1]) * scale
        dks = pltpu.roll(jnp.where(low, dk[0], dk[1]) * scale, 64, 1)
        dvs = jnp.where(low, dv[0], dv[1])
        act_own[s, :, span(p * 384, 128)] = jnp.where(low, dqs, dks).astype(BF)
        act_own[s, :, span(p * 384 + 128, 128)] = jnp.where(low, dvs, dqs).astype(BF)
        act_own[s, :, span(p * 384 + 256, 128)] = jnp.where(low, dks, dvs).astype(BF)

    def send_qkv(s):
        return net.send(act_own.at[s, :, pl.ds(0, 768)], slope.at[s, :, pl.ds(0, 768)], twin)

    net.drain(act_got.values())
    for c in range(CHUNKS):
        ga_sent[c][1].wait_recv()
    sum1.advance(0)
    context_back(0)
    back_pair(0, 0)
    back_pair(0, 1)
    dqkv_got = [send_qkv(0)]
    passed = [pass_on(grad_attn, c, ga_sent[c][0]) for c in range(CHUNKS)]
    for copy in passed:
        copy.wait_recv()
    context_back(1)
    back_pair(1, 0)
    sum1.advance(1)
    back_pair(1, 1)
    dqkv_got.append(send_qkv(1))

    for part, ctx in enumerate((ctx_own, ctx_o)):
        side = n if part == 0 else 1 - n
        got = mm_left(ctx[0], ga_own[0]) + mm_left(ctx[1], ga_own[1])
        packed[span(OUT_BASE + side * 256, 256), :] = got.astype(BF)
    for s in range(2):
        column_add(SMALL_OUT, ga_own[s].astype(F32))
    sum1.advance(2)
    dqkv_got[0].wait_recv()
    dqkv_got[1].wait_recv()
    for part, g in enumerate((act_own, slope)):
        side = n if part == 0 else 1 - n

        def qkv_block(j):
            cols = span(j * 256, 256)
            got = mm_left(g[0, :, cols], hid[span(base_of[0], SEQ), :]) + mm_left(
                g[1, :, cols], hid[span(base_of[1], SEQ), :]
            )
            packed[span(QKV_BASE + side * 768 + j * 256, 256), :] = got.astype(BF)

        tiles(3, qkv_block)

        def qkv_bias(j):
            cols = span(j * 256, 256)
            total = jnp.sum(g[0, :, cols].astype(F32), 0, keepdims=True) + jnp.sum(
                g[1, :, cols].astype(F32), 0, keepdims=True
            )
            small[pl.ds(SMALL_QKV + side * 3 + j, 1), :] = total

        tiles(3, qkv_bias)
    sum2 = Summing(
        packed,
        lambda q, place, size: act_o.at[q // 2, pl.ds(place, size), pl.ds((q % 2) * 512, 512)],
        fin, attention_out, (ss2, rs2_sem, ls2), UP_ROWS + DOWN_ROWS, QKV_ROWS + OUT_ROWS, 256, table,
    )
    sum2.open()
    smalls = SmallSum(small, small_kept, small_recv, (small_ss, small_rs), table)
    smalls.begin(0)

    def input_rows(s, c):
        here = pl.ds(c * PART, PART)
        return mm(act_own[s, here, 0:768], qkv_w[span(n * 768, 768), :]) + mm(
            slope[s, here, 0:768], qkv_w[span((1 - n) * 768, 768), :]
        )

    sum1.advance(3)
    for c in range(CHUNKS):
        reduce_send(3, c, input_rows(1, c))
    for c in range(CHUNKS):
        acc[pl.ds(c * PART, PART), :] = input_rows(0, c)
    smalls.take(0)
    sum2.advance(0)
    sum1.advance(4)
    smalls.take(1)
    sum2.advance(1)
    sum1.advance(5)
    sum2.advance(2)
    smalls.take(2)
    for c in range(CHUNKS):
        rs_sent[3, c].wait_recv()

        def finish(i):
            rows = span(c * PART + i * STEP, STEP, 64)
            in_grad[rows, :] = res2[rows, :] + acc[rows, :] + rs_recv[1, rows, :].astype(F32)

        tiles(PART // STEP, finish)
    sum1.advance(6)
    sum2.advance(3)
    smalls.take(3)
    sum2.advance(4)
    smalls.take(4)
    sum2.advance(5)
    sum1.advance(7)
    smalls.take(5)
    sum2.advance(6)
    sum2.advance(7)
    sum1.advance(8)
    sum2.advance(8)
    for work in (net, sum1, sum2, smalls):
        work.close()


def layer_call(*arrays):
    vmem = pl.BlockSpec(memory_space=pltpu.VMEM)
    anywhere = pl.BlockSpec(memory_space=pl.ANY)
    shapes = [
        ((2, SEQ, 512), BF), ((768, 512), BF), ((256, 512), BF), ((512, 1024), BF), ((1024, 512), BF),
        ((2, 2, SEQ, 128), BF), ((2, 2, SEQ, 128), BF), ((2, 2, SEQ, 128), BF),
        ((2, 4, SEQ, SEQ), BF), ((2, SEQ, 256), BF), ((2, SEQ, 256), BF),
        ((2, SEQ, 512), BF), ((2, SEQ, 512), BF), ((3, SEQ, 128), F32), ((3, SEQ, 128), F32),
        ((SEQ, 512), F32), ((SEQ, 512), F32), ((SEQ, 512), F32), ((SEQ, 128), F32), ((PART, 1024), F32),
        ((2, SEQ, 512), BF), ((2, SEQ, 512), BF), ((2, SEQ, 1024), BF), ((2, SEQ, 1024), BF),
        ((2, SEQ, 1024), BF), ((2, SEQ, 512), BF), ((2, SEQ, 512), BF), ((2, SEQ, 1024), BF),
        ((2, SEQ, 1024), BF), ((2, SEQ, 512), BF), ((2, SEQ, 512), BF),
        ((SEQ, 256), BF), ((PACKED_ROWS, PACK), BF), ((4, 1024, PACK), BF), ((384, PACK), BF),
        ((6, ROWS_SMALL, 256), F32), ((6, ROWS_SMALL, 256), F32),
    ]
    return pl.pallas_call(
        layer_kernel,
        out_shape=(
            jax.ShapeDtypeStruct((SEQ, 512), BF),
            jax.ShapeDtypeStruct((SEQ, 512), F32),
            jax.ShapeDtypeStruct((QKV_ROWS, PACK), BF),
            jax.ShapeDtypeStruct((OUT_ROWS, PACK), BF),
            jax.ShapeDtypeStruct((512, UP_ROWS), BF),
            jax.ShapeDtypeStruct((DOWN_ROWS, PACK), BF),
            jax.ShapeDtypeStruct((ROWS_SMALL, 256), F32),
        ),
        in_specs=[anywhere if i in (4, 8, 10, 14) else vmem for i in range(len(arrays))],
        out_specs=(vmem, vmem) + (anywhere,) * 4 + (vmem,),
        scratch_shapes=[
            pltpu.VMEM((512, 512), BF),
            pltpu.VMEM((512, 2048), BF),
            pltpu.VMEM((2048, 512), BF),
            pltpu.VMEM((512, 512), BF),
            pltpu.SemaphoreType.DMA((4,)),
        ]
        + [pltpu.VMEM(*shape) for shape in shapes]
        + [
            pltpu.SemaphoreType.DMA(shape)
            for shape in (
                (MESSAGES,), (MESSAGES,), (4, 9), (4, 9), (4,), (4, 9), (4, 9), (4,), (6,), (6,)
            )
        ],
        compiler_params=pltpu.CompilerParams(
            collective_id=2, has_side_effects=True, vmem_limit_bytes=60 * 2**20
        ),
    )(*arrays)


def finish_kernel(
    hidden, grad, qkv, out, up, down, small,
    hidden_o, grad_o, qkv_o, out_o, up_o, down_o, qvb_o, outb_o, upb_o, downb_o, g1_o, s1_o, g2_o, s2_o,
):
    hidden_o[...] = hidden[...]
    grad_o[...] = grad[...]
    qkv_o[...] = qkv[...].astype(F32)
    out_o[...] = out[...].astype(F32)
    up_o[...] = up[...].astype(F32)
    down_o[...] = down[...].astype(F32)

    @pl.when(pl.program_id(0) == 0)
    def _():
        for head in range(8):
            for i in range(2):
                row, lane = divmod(head * 192 + i * 128, 256)
                row += SMALL_QKV
                qvb_o[head, i : i + 1, :] = small[row : row + 1, lane : lane + 64]
        bases = [SMALL_NORM + 2 * i for i in range(4)]
        for ref, first, count in (
            (outb_o, SMALL_OUT, 2),
            (upb_o, SMALL_UP, 8),
            (downb_o, SMALL_DOWN, 2),
            (g1_o, bases[0], 2),
            (s1_o, bases[1], 2),
            (g2_o, bases[2], 2),
            (s2_o, bases[3], 2),
        ):
            for j in range(count):
                ref[:, j * 256 : (j + 1) * 256] = small[first + j : first + j + 1, :]


def finish_call(hidden, grad, qkv, out, up, down, small):
    steps = 16

    def rows(shape):
        return pl.BlockSpec((shape[0] // steps, shape[1]), lambda i: (i, 0))

    def whole(shape):
        return pl.BlockSpec(shape, lambda i: (0,) * len(shape))

    big = [hidden, grad, qkv, out, up, down]
    thin = [(8, 2, 64), (1, 512), (1, 2048), (1, 512)] + [(1, 512)] * 4
    return pl.pallas_call(
        finish_kernel,
        grid=(steps,),
        out_shape=[
            jax.ShapeDtypeStruct(a.shape, BF if a is hidden else F32) for a in big
        ]
        + [jax.ShapeDtypeStruct(shape, F32) for shape in thin],
        in_specs=[rows(a.shape) for a in big] + [whole(small.shape)],
        out_specs=[rows(a.shape) for a in big] + [whole(shape) for shape in thin],
        compiler_params=pltpu.CompilerParams(vmem_limit_bytes=60 * 2**20),
    )(*big, small)


def per_device(
    hidden_in,
    segment_ids,
    qkv_weight,
    qv_bias,
    out_weight,
    out_bias,
    norm1_gain,
    norm1_shift,
    up_weight,
    up_bias,
    down_weight,
    down_bias,
    norm2_gain,
    norm2_shift,
    out_grad,
):
    half_width = hidden_in.shape[1]
    heads_here, head_width = qkv_weight.shape[1], qkv_weight.shape[3]
    results = layer_call(
        hidden_in,
        segment_ids.reshape(-1, 128),
        qkv_weight.transpose(1, 2, 3, 0).reshape(-1, half_width),
        qv_bias,
        out_weight.reshape(-1, half_width),
        out_bias[None],
        norm1_gain[None],
        norm1_shift[None],
        up_weight,
        up_bias[None],
        down_weight,
        down_bias[None],
        norm2_gain[None],
        norm2_shift[None],
        out_grad,
    )

    hidden_out, input_grad, qkv, out, up, down, qv, outb, upb, downb, *norms = finish_call(*results)
    return (
        hidden_out,
        input_grad,
        qkv.reshape(heads_here, 3, head_width, half_width).transpose(3, 0, 1, 2),
        qv,
        out.reshape(heads_here, head_width, half_width),
        outb.reshape(-1),
        norms[0].reshape(-1),
        norms[1].reshape(-1),
        up,
        upb.reshape(-1),
        down,
        downb.reshape(-1),
        norms[2].reshape(-1),
        norms[3].reshape(-1),
    )


def solution(mesh):
    return jax.shard_map(
        per_device,
        mesh=mesh,
        in_specs=(
            P("dp", "narrow"),
            P("dp"),
            P("narrow", "wide", None, None),
            P("wide", None, None),
            P("wide", None, "narrow"),
            P("narrow"),
            P("narrow"),
            P("narrow"),
            P("narrow", "wide"),
            P("wide"),
            P("wide", "narrow"),
            P("narrow"),
            P("narrow"),
            P("narrow"),
            P(("dp", "wide"), "narrow"),
        ),
        out_specs=(
            P(("dp", "wide"), "narrow"),
            P(("dp", "wide"), "narrow"),
            P("narrow", "wide", None, None),
            P("wide", None, None),
            P("wide", None, "narrow"),
            P("narrow"),
            P("narrow"),
            P("narrow"),
            P("narrow", "wide"),
            P("wide"),
            P("wide", "narrow"),
            P("narrow"),
            P("narrow"),
            P("narrow"),
        ),
        check_vma=False,
    )
```
